32 devices in a mesh: phase: 2 (over x), ctx: 16 (over z, y, core).
Axes of the slice: x: 2, y: 2, z: 4, core: 2. Of those that a mesh axis runs over, the one named last changes fastest.
Arguments:
- inputs: bfloat16 [1, 2048, 2048], P(None, 'ctx'), may hold values from -6 to 6
- segment_ids: int32 [1, 2048], P(None, 'ctx'), may hold values from 0 to 7, never falling along the last dimension, each value on 1 to 768 neighbouring positions
- w_query: bfloat16 [2, 2048, 1024], P('phase'), may hold values from -1 to 1
- w_keyval: bfloat16 [2, 2048, 2048], P('phase', 'ctx'), may hold values from -16 to 16
- w_out: bfloat16 [2, 1024, 2048], P('phase'), may hold values from -0.1875 to 0.1875
Outputs:
- section_out: bfloat16 [2, 1, 2048, 2048], P('phase', None, 'ctx')
The draws below stay inside these ranges and needn't reach their ends.
Inputs may be any that keep to these rules, and one draw needn't show every extreme that they name: `segment_ids`: ids never fall along the tokens of a micro-batch; each trajectory is a run of 1 to 768 tokens and one run has exactly 768.
All inputs are finite; a program needn't handle non-finite values.
Results may differ from the reference program's by a relative error of at most 0.015.
Values may be sent and summed in bfloat16 or wider, within the bound.
No kernel may reach another device: no remote copies, remote signals or barrier semaphores. Data moves between devices by JAX's collectives and lax.ppermute only.
A program may use at most 64 MiB of HBM per device.

```python
import math
import jax
import jax.numpy as jnp
import numpy as np
from jax import lax

D = 2048
HEADS = 8
HEAD = 128
WINDOW = 4
TOK_DEV = 128
MB = 1
LAYERS = 2
TOKENS = 2048
SEGS = 8
SEG_MOST = 768
N_CTX = 16


def shared_query(key):
    base = jax.random.normal(jax.random.fold_in(key, 11), (LAYERS, D, HEADS * HEAD), jnp.float32)
    return base / math.sqrt(D)


def draw_w_query(key, part):
    return shared_query(key).astype(jnp.bfloat16)


def draw_w_keyval(key, part):
    head_width = HEADS * HEAD
    fresh = jax.random.normal(jax.random.fold_in(key, 23), (LAYERS, D, 2 * head_width), jnp.float32) / math.sqrt(D)
    return fresh.astype(jnp.bfloat16)


def block_scale(own_key, shape, pieces, low, largest):
    def one(position, blocks):
        heights = jax.random.uniform(jax.random.fold_in(jax.random.fold_in(own_key, 6), position), (blocks,), jnp.float32, low / len(pieces), largest / len(pieces))
        return jnp.repeat(jnp.exp(heights), shape[position] // blocks).reshape((-1,) + (1,) * (len(shape) - position - 1))

    factor_of = one(*pieces[0])
    for cut in pieces[1:]:
        factor_of = factor_of * one(*cut)
    return factor_of


def split_up(count, total, limit, lean):
    portions = [(1 << 20) // math.isqrt(rank ** lean) + 1 for rank in range(2, count + 1)]
    surplus, given = total - limit - (count - 1), [1] * (count - 1)
    while surplus > 0:
        candidates = [i for i in range(count - 1) if given[i] < limit]
        whole, budget = sum([portions[i] for i in candidates]), surplus
        for i in candidates:
            more = min(limit - given[i], max(1, budget * portions[i] // whole), surplus)
            given[i] = given[i] + more
            surplus = surplus - more
    return np.array([limit] + given)


def uneven(rng, amount, total, limit, slope):
    if amount == 2:
        one = jax.random.randint(rng, (), max(1, total - limit), min(limit, total - 1) + 1)
        return jnp.stack([one, total - one])
    lengths = jnp.asarray(split_up(amount, total, limit, slope), jnp.int32)
    pairs = (amount - 1) // 2
    giver, receiver = lengths[1:1 + 2 * pairs:2], lengths[2:2 + 2 * pairs:2]
    room = jnp.minimum(giver - 1, limit - receiver)
    passed = jax.random.randint(jax.random.fold_in(rng, 1), (pairs,), 0, 1 << 20) % (room + 1)
    lengths = lengths.at[1:1 + 2 * pairs:2].set(giver - passed).at[2:2 + 2 * pairs:2].set(receiver + passed)
    return lengths[jax.random.permutation(jax.random.fold_in(rng, 2), amount)]


def bell_draw(own_key, dims, deviation, reach, split=(), kind=jnp.bfloat16):
    drawn = jax.random.normal(own_key, dims, jnp.float32) * deviation
    if len(split) > 0:
        drawn = block_scale(own_key, dims, split, -0.22, 0.18) * drawn
    return jnp.clip(drawn, min=-reach, max=reach).astype(kind)


def setup_inputs(seed: int = 0) -> dict:
    splits = jax.random.split(jax.random.key(seed), 6)
    inputs = bell_draw(splits[0], (MB, TOKENS, D), 1.0, 6.0, ((1, 16),))
    segment_ids = jax.vmap(lambda own: jnp.searchsorted(jnp.cumsum(uneven(own, SEGS, TOKENS, SEG_MOST, 0)), jnp.arange(TOKENS), side="right"))(jax.random.split(splits[1], MB)).reshape((MB, TOKENS)).astype(jnp.int32)
    w_query = draw_w_query(jax.random.fold_in(splits[5], 71), 0)
    w_keyval = draw_w_keyval(jax.random.fold_in(splits[5], 71), 0)
    w_out = bell_draw(splits[4], (LAYERS, HEADS * HEAD, D), (HEADS * HEAD) ** -0.5, 0.1875, ((0, 2),))
    return dict(inputs=inputs, segment_ids=segment_ids, w_query=w_query, w_keyval=w_keyval, w_out=w_out)


def rms_rows(values):
    widened = values.astype(jnp.float32)
    return (widened * lax.rsqrt(lax.optimization_barrier(jnp.mean(widened * widened, axis=-1, keepdims=True)) + 1e-05)).astype(jnp.bfloat16)

def segment_begin(segments):
    places = jnp.arange(segments.shape[0], dtype=jnp.int32)
    earlier = jnp.concatenate([jnp.full((1,), -1, jnp.int32), segments[:-1]])
    boundary = jnp.where(segments != earlier, places, jnp.zeros_like(places))
    return lax.cummax(boundary, axis=0)

def layer_pass(stream, segments, query_w, keyval_w, out_w):
    normed = rms_rows(stream)
    queries = jnp.dot(normed, query_w, preferred_element_type=jnp.float32).astype(jnp.bfloat16)
    keyvals = jnp.dot(normed, keyval_w, preferred_element_type=jnp.float32).astype(jnp.bfloat16)
    queries = lax.optimization_barrier(queries)
    keyvals = lax.optimization_barrier(keyvals)
    begins = segment_begin(segments)
    head_width = HEADS * HEAD
    padded = jnp.concatenate([jnp.zeros(((WINDOW - 1) * TOK_DEV, 2 * head_width), jnp.bfloat16), keyvals], axis=0)
    score_scale = 1.0 / math.sqrt(HEAD)

    def query_block(block_index):
        first_pos = (block_index * TOK_DEV).astype(jnp.int32)
        query_part = lax.dynamic_slice_in_dim(queries, first_pos, TOK_DEV, 0).reshape(TOK_DEV, HEADS, HEAD).astype(jnp.float32)
        key_rows = lax.dynamic_slice_in_dim(padded, first_pos, WINDOW * TOK_DEV, 0)
        key_part = key_rows[:, :head_width].reshape(-1, HEADS, HEAD).astype(jnp.float32)
        value_part = key_rows[:, head_width:].reshape(-1, HEADS, HEAD).astype(jnp.float32)
        scores = jnp.einsum('qhd,khd->hqk', query_part, key_part) * score_scale
        query_pos = first_pos + jnp.arange(TOK_DEV, dtype=jnp.int32)
        key_pos = first_pos - (WINDOW - 1) * TOK_DEV + jnp.arange(WINDOW * TOK_DEV, dtype=jnp.int32)
        begin_part = lax.dynamic_slice_in_dim(begins, first_pos, TOK_DEV, 0)
        allowed = (key_pos[None, :] <= query_pos[:, None]) & (key_pos[None, :] >= begin_part[:, None])
        scores = jnp.where(allowed[None], scores, -jnp.inf)
        row_top = lax.optimization_barrier(jnp.max(scores, axis=2, keepdims=True))
        weights = jnp.exp(scores - row_top)
        weights = (weights / lax.optimization_barrier(jnp.sum(weights, axis=2, keepdims=True))).astype(jnp.bfloat16)
        weights = lax.optimization_barrier(weights)
        blended = jnp.einsum('hqk,khd->qhd', weights.astype(jnp.float32), value_part)
        return blended.astype(jnp.bfloat16).reshape(TOK_DEV, head_width)
    blocks = lax.map(query_block, jnp.arange(N_CTX, dtype=jnp.int32))
    heads_out = blocks.reshape(TOKENS, head_width)
    update = jnp.dot(heads_out, out_w, preferred_element_type=jnp.float32)
    return (stream.astype(jnp.float32) + update).astype(jnp.bfloat16)

def reference(inputs, segment_ids, w_query, w_keyval, w_out):
    layers_out = []
    for layer_index in range(LAYERS):
        batch_out = []
        for batch_index in range(MB):
            if layer_index == 0:
                stream = inputs[batch_index]
            else:
                stream = layers_out[-1][batch_index]
            batch_out.append(layer_pass(stream, segment_ids[batch_index], w_query[layer_index], w_keyval[layer_index], w_out[layer_index]))
        layers_out.append(jnp.stack(batch_out))
    return jnp.stack(layers_out)
```

```python
import functools
import math

import jax
import jax.numpy as jnp
from jax import lax
from jax.experimental import pallas as pl
from jax.experimental.pallas import tpu as pltpu
from jax.sharding import PartitionSpec as P

HEAD = 128
WINDOW = 4
PLANE = 4
ORDER = (0, 2, 1, 3)
BOTH = ("phase", "ctx")
VMEM_BYTES = 48 * 1024 * 1024


def swap(block, phase_bit, ctx_bits):
    wide = lax.axis_size("ctx")
    route = [
        (f * wide + d, (f ^ phase_bit) * wide + (d ^ ctx_bits))
        for f in range(lax.axis_size("phase"))
        for d in range(wide)
    ]
    return lax.ppermute(block, BOTH, route)


def from_plane_behind(block):
    wide = lax.axis_size("ctx")
    return lax.ppermute(block, "ctx", [(i, i + PLANE) for i in range(wide - PLANE)])


def pick(blocks, index):
    return lax.dynamic_index_in_dim(blocks, index, 0, keepdims=False)


def rms_rows(values):
    widened = values.astype(jnp.float32)
    scale = lax.rsqrt(jnp.mean(widened * widened, axis=-1, keepdims=True) + 1e-05)
    return (widened * scale).astype(jnp.bfloat16)


def dot(a, b):
    return jnp.dot(a, b, preferred_element_type=jnp.float32)


def call(kernel, outs, scratch, flops, *operands):
    moved = sum(o.size * o.dtype.itemsize for o in operands)
    return pl.pallas_call(
        kernel,
        out_shape=[jax.ShapeDtypeStruct(s, d) for s, d in outs],
        in_specs=[pl.BlockSpec(memory_space=pltpu.VMEM)] * len(operands),
        out_specs=[pl.BlockSpec(memory_space=pltpu.VMEM)] * len(outs),
        scratch_shapes=[pltpu.VMEM(s, d) for s, d in scratch],
        cost_estimate=pl.CostEstimate(flops=flops, bytes_accessed=moved, transcendentals=0),
        compiler_params=pltpu.CompilerParams(vmem_limit_bytes=VMEM_BYTES),
    )(*operands)


def fill_weights(ctx, weight_refs, weights):
    rows = weight_refs[0].shape[0] // PLANE
    for m, ref in enumerate(weight_refs):
        for r, o in enumerate(ORDER):
            source = ctx ^ (PLANE * m + o)
            weights[pl.ds(pl.multiple_of(source * rows, rows), rows), :] = ref[
                r * rows : (r + 1) * rows, :
            ]


def project(normed, weights, wq_ref, q_ref, kv_ref, tail_ref):
    rows = tail_ref.shape[0]
    keyvals = dot(normed[...], weights[...]).astype(jnp.bfloat16)
    kv_ref[...] = keyvals
    tail_ref[...] = keyvals[keyvals.shape[0] - rows :]
    q_ref[...] = dot(normed[...], wq_ref[...]).astype(jnp.bfloat16)


def first_kernel(pieces, *refs):
    x_refs, weight_refs = refs[:PLANE], refs[PLANE : PLANE + pieces]
    wq_ref, q_ref, kv_ref, tail_ref, normed, weights = refs[PLANE + pieces :]
    ctx = lax.axis_index("ctx")
    rows = x_refs[0].shape[0]
    own = lax.rem(ctx, PLANE)
    for r, o in enumerate(ORDER):
        normed[pl.ds(pl.multiple_of((own ^ o) * rows, rows), rows), :] = rms_rows(x_refs[r][...])
    fill_weights(ctx, weight_refs, weights)
    project(normed, weights, wq_ref, q_ref, kv_ref, tail_ref)


def second_kernel(pieces, *refs):
    x_refs, b_refs = refs[:PLANE], refs[PLANE : 3 * PLANE]
    wo_refs, refs = refs[3 * PLANE : 4 * PLANE], refs[4 * PLANE :]
    weight_refs, refs = refs[:pieces], refs[pieces:]
    wq_ref, own_ref, q_ref, kv_ref, tail_ref, stream, blended, normed, weights = refs
    ctx = lax.axis_index("ctx")
    side = lax.rem(lax.axis_index("phase"), 2)
    rows = x_refs[0].shape[0]
    own = lax.rem(ctx, PLANE)
    part = b_refs[0].shape[1]
    deep = wo_refs[0].shape[0]
    fill_weights(ctx, weight_refs, weights)
    for r, o in enumerate(ORDER):
        stream[pl.ds(pl.multiple_of((own ^ o) * rows, rows), rows), :] = x_refs[r][...]
    for m, ref in enumerate(b_refs):
        place = (side * PLANE + own) ^ m
        blended[:, pl.ds(pl.multiple_of(place * part, part), part)] = ref[...]
    width = stream.shape[1]
    step = min(512, width)
    for n in range(0, width, step):
        total = stream[:, n : n + step].astype(jnp.float32)
        for r, o in enumerate(ORDER):
            place = pl.multiple_of((own ^ o) * deep, deep)
            total = total + dot(blended[:, pl.ds(place, deep)], wo_refs[r][:, n : n + step])
        stream[:, n : n + step] = total.astype(jnp.bfloat16)
    normed[...] = rms_rows(stream[...])
    own_ref[...] = stream[pl.ds(pl.multiple_of(own * rows, rows), rows), :]
    project(normed, weights, wq_ref, q_ref, kv_ref, tail_ref)


def mask_kernel(rows, id_ref, past_ref, bias_ref):
    ctx = lax.axis_index("ctx")
    own = lax.rem(ctx, PLANE)
    first = ctx < PLANE

    def ids(group):
        ref = id_ref if group >= WINDOW - 1 else past_ref
        natural = group - (WINDOW - 1) if group >= WINDOW - 1 else group + PLANE - (WINDOW - 1)
        row = jnp.zeros((1, rows), jnp.int32)
        for r, o in enumerate(ORDER):
            row = row + jnp.where((own ^ o) == natural, 1, 0) * ref[r : r + 1, :]
        return row

    keys = [ids(t) for t in range(PLANE + WINDOW - 1)]
    causal = lax.broadcasted_iota(jnp.int32, (rows, rows), 0) >= lax.broadcasted_iota(
        jnp.int32, (rows, rows), 1
    )
    for g in range(PLANE):
        mine = keys[g + WINDOW - 1].astype(jnp.float32)
        mine = jnp.transpose(jnp.broadcast_to(mine, (rows, rows)))
        for t in range(WINDOW):
            allowed = mine == keys[g + t].astype(jnp.float32)
            if t == WINDOW - 1:
                allowed = allowed & causal
            if g + t < WINDOW - 1:
                allowed = allowed & jnp.logical_not(first)
            bias_ref[g, :, t * rows : (t + 1) * rows] = jnp.where(allowed, 0.0, -jnp.inf)


def attend_kernel(split, q_ref, kv_ref, past_ref, bias_ref, *refs):
    out_refs, window = refs[:-1], refs[-1]
    rows = bias_ref.shape[1]
    past = past_ref.shape[0]
    part = q_ref.shape[1]
    window[:past] = past_ref[...]
    window[past:] = kv_ref[...]
    upper = lax.rem(lax.axis_index("ctx"), PLANE) // 2
    for g in range(PLANE):
        keys = window[g * rows : (g + WINDOW) * rows]
        for h in range(0, part, HEAD):
            query = q_ref[g * rows : (g + 1) * rows, h : h + HEAD]
            scores = lax.dot_general(
                query, keys[:, h : h + HEAD], (((1,), (1,)), ((), ())),
                preferred_element_type=jnp.float32,
            )
            scores = scores * (1.0 / math.sqrt(HEAD)) + bias_ref[g]
            weights = jnp.exp(scores - jnp.max(scores, axis=1, keepdims=True))
            total = jnp.sum(weights, axis=1, keepdims=True)
            values = keys[:, part + h : part + h + HEAD]
            result = (dot(weights.astype(jnp.bfloat16), values) / total).astype(jnp.bfloat16)
            if not split:
                out_refs[0][g * rows : (g + 1) * rows, h : h + HEAD] = result
                continue
            place = (g % 2) * rows

            def put(ref):
                ref[place : place + rows, h : h + HEAD] = result

            pl.when(upper == g // 2)(functools.partial(put, out_refs[0]))
            pl.when(upper != g // 2)(functools.partial(put, out_refs[1]))


def last_kernel(*refs):
    b_refs, (wo_ref, own_ref, out_ref, blended) = refs[: 2 * PLANE], refs[2 * PLANE :]
    own = lax.rem(lax.axis_index("ctx"), PLANE)
    side = lax.rem(lax.axis_index("phase"), 2)
    rows, part = own_ref.shape[0], b_refs[0].shape[1]

    @pl.when(side == 0)
    def _():
        out_ref[...] = own_ref[...]

    @pl.when(side == 1)
    def _():
        for m, ref in enumerate(b_refs):
            place = (side * PLANE + own) ^ m
            start = pl.multiple_of(lax.rem(own, 2) * rows, rows)
            blended[:, pl.ds(pl.multiple_of(place * part, part), part)] = ref[pl.ds(start, rows), :]
        total = own_ref[...].astype(jnp.float32) + dot(blended[...], wo_ref[...])
        out_ref[...] = total.astype(jnp.bfloat16)


def plane_rows(block):
    across = swap(block, 0, 2)
    return [block, across, swap(block, 0, 1), swap(across, 0, 1)]


def key_weights(blocks, own):
    upper, core = own // 2, own % 2
    pairs = blocks.reshape((2, 2) + blocks.shape[1:])
    kept = pick(pairs, upper)
    got = swap(pick(pairs, 1 - upper), 0, 2)
    near = [pick(kept, core), pick(got, core)]
    far = swap(jnp.stack([pick(kept, 1 - core), pick(got, 1 - core)]), 0, 1)
    piece = jnp.concatenate(near + [far[0], far[1]], axis=0)
    count = lax.axis_size("ctx") // PLANE
    return [piece] + [swap(piece, 0, PLANE * m) for m in range(count - 1, 0, -1)][::-1]


def local(inputs, segment_ids, w_query, w_keyval, w_out):
    batches, rows, width = inputs.shape
    phases = lax.axis_size("phase")
    phase = lax.axis_index("phase")
    side = phase % 2
    ctx = lax.axis_index("ctx")
    own = ctx % PLANE
    bf16 = jnp.bfloat16

    head_width = w_query.shape[2]
    part = head_width // (2 * PLANE)
    depth = w_keyval.shape[1]
    blocks = w_keyval[0].reshape(depth, 2, 2 * PLANE, part).transpose(2, 0, 1, 3)
    blocks = blocks.reshape(2, PLANE, depth, 2 * part)
    kept, got = pick(blocks, side), swap(pick(blocks, 1 - side), 1, 0)
    early = key_weights(jnp.where(side == 0, kept, got), own)
    late = key_weights(jnp.where(side == 0, got, kept), own)

    mat = w_query[0]
    kept = lax.dynamic_slice_in_dim(mat, (side * PLANE + own) * part, part, 1)
    sent = lax.dynamic_slice_in_dim(mat, ((1 - side) * PLANE + own) * part, part, 1)
    got = swap(sent, 1, 0)
    early_query, late_query = jnp.where(side == 0, kept, got), jnp.where(side == 0, got, kept)

    mat = w_out[0]
    quarter = head_width // PLANE
    kept = lax.dynamic_slice_in_dim(mat, own * quarter, quarter, 0)
    early_out = plane_rows(jnp.where(side == 0, kept, swap(kept, 1, 0)))

    tall, past = PLANE * rows, (WINDOW - 1) * rows
    pieces = len(early)
    qkv = [((tall, part), bf16), ((tall, 2 * part), bf16), ((past, 2 * part), bf16)]
    weights = ((width, 2 * part), bf16)
    qkv_flops = 2 * tall * width * 3 * part
    attend_flops = 4 * tall * WINDOW * rows * part
    window = [((past + tall, 2 * part), bf16)]

    def bias_of(ids):
        plane = jnp.concatenate([ids, swap(ids, 0, 2)], axis=0)
        plane = jnp.concatenate([plane, swap(plane, 0, 1)], axis=0)
        shape = ((PLANE, rows, WINDOW * rows), jnp.float32)
        return call(
            functools.partial(mask_kernel, rows), [shape], [], 0, plane, from_plane_behind(plane)
        )[0]

    biases = [bias_of(segment_ids[b : b + 1]) for b in range(batches)]

    def two_layers(x, bias):
        xs = plane_rows(x)
        q, kv, tail = call(
            functools.partial(first_kernel, pieces), qkv, [((tall, width), bf16), weights],
            qkv_flops, *xs, *early, early_query,
        )
        blended = call(
            functools.partial(attend_kernel, False), [((tall, part), bf16)], window,
            attend_flops, q, kv, from_plane_behind(tail), bias,
        )[0]
        near = [blended, swap(blended, 0, 2), swap(blended, 1, 0), swap(blended, 1, 2)]
        heads = [b for n in near for b in (n, swap(n, 0, 1))]
        stream, q, kv, tail = call(
            functools.partial(second_kernel, pieces), [((rows, width), bf16)] + qkv,
            [((tall, width), bf16), ((tall, head_width), bf16), ((tall, width), bf16), weights],
            qkv_flops + 2 * tall * head_width * width,
            *xs, *heads, *early_out, *late, late_query,
        )
        mine, other = call(
            functools.partial(attend_kernel, True), [((tall // 2, part), bf16)] * 2, window,
            attend_flops, q, kv, from_plane_behind(tail), bias,
        )
        near = [mine, swap(other, 0, 2), swap(mine, 1, 0), swap(other, 1, 2)]
        heads = [b for n in near for b in (n, swap(n, 0, 1))]
        return call(
            last_kernel, [((rows, width), bf16)], [((rows, head_width), bf16)],
            2 * rows * head_width * width, *heads, w_out[0], stream,
        )[0]

    outs = []
    for b in range(batches):
        x, out = inputs[b], None
        for tick in range(phases // 2):
            result = two_layers(x, biases[b])
            out = result if out is None else jnp.where(phase // 2 == tick, result, out)
            if tick + 1 < phases // 2:
                ahead = [
                    lax.ppermute(result, "phase", [(f, f + d) for f in range(1, phases - d, 2)])
                    for d in (1, 2)
                ]
                x = jnp.where(side == 0, ahead[0], ahead[1])
        outs.append(out)
    return jnp.stack(outs)[None]


def solution(mesh):
    placed = (
        P(None, "ctx", None),
        P(None, "ctx"),
        P("phase", None, None),
        P("phase", "ctx", None),
        P("phase", None, None),
    )
    return jax.shard_map(
        local, mesh=mesh, in_specs=placed, out_specs=P("phase", None, "ctx", None), check_vma=False
    )
```

```python
import functools
import math

import jax
import jax.numpy as jnp
from jax import lax
from jax.experimental import pallas as pl
from jax.experimental.pallas import tpu as pltpu
from jax.sharding import PartitionSpec as P

HEAD = 128
WINDOW = 4
PLANE = 4
ORDER = (0, 2, 1, 3)
BOTH = ("phase", "ctx")
VMEM_BYTES = 24 * 1024 * 1024
LONG = 10**11


def swap(block, phase_bit, ctx_bits):
    wide = lax.axis_size("ctx")
    route = [
        (f * wide + d, (f ^ phase_bit) * wide + (d ^ ctx_bits))
        for f in range(lax.axis_size("phase"))
        for d in range(wide)
    ]
    return lax.ppermute(block, BOTH, route)


def from_plane_behind(block):
    wide = lax.axis_size("ctx")
    return lax.ppermute(block, "ctx", [(i, i + PLANE) for i in range(wide - PLANE)])


def rms_rows(values):
    widened = values.astype(jnp.float32)
    scale = lax.rsqrt(jnp.mean(widened * widened, axis=-1, keepdims=True) + 1e-05)
    return (widened * scale).astype(jnp.bfloat16)


def dot(a, b):
    return jnp.dot(a, b, preferred_element_type=jnp.float32)


def call(kernel, outs, scratch, flops, *operands, far=()):
    moved = sum(o.size * o.dtype.itemsize for o in operands)
    place = lambda i: pltpu.HBM if i in far else pltpu.VMEM
    return pl.pallas_call(
        kernel,
        out_shape=[jax.ShapeDtypeStruct(s, d) for s, d in outs],
        in_specs=[pl.BlockSpec(memory_space=place(i)) for i in range(len(operands))],
        out_specs=[pl.BlockSpec(memory_space=pltpu.VMEM)] * len(outs),
        scratch_shapes=[pltpu.VMEM(*s) if isinstance(s, tuple) else s for s in scratch],
        cost_estimate=pl.CostEstimate(flops=flops, bytes_accessed=moved, transcendentals=0),
        compiler_params=pltpu.CompilerParams(vmem_limit_bytes=VMEM_BYTES),
    )(*operands)


def extend_kernel(x_ref, id_ref, out_ref):
    rows, width = x_ref.shape
    lanes = out_ref.shape[1] - width
    out_ref[:, :width] = x_ref[...]
    ids = jnp.broadcast_to(id_ref[...].astype(jnp.float32), (rows, rows))
    out_ref[:, width:] = jnp.broadcast_to(
        jnp.transpose(ids)[:, :1], (rows, lanes)
    ).astype(jnp.bfloat16)


def slice_kernel(out_ref, query_ref, sent_out, query_mat, sems):
    side = lax.rem(lax.axis_index("phase"), 2)
    own = lax.rem(lax.axis_index("ctx"), PLANE)
    half, part = sent_out.shape[0] // 3, query_mat.shape[1] // 2
    copies = []
    for i, (first, count, place) in enumerate(((0, 2, 2 * own), (2, 1, 2 * (own ^ 2)))):
        at = pl.ds(pl.multiple_of(place * half, half), count * half)
        to = sent_out.at[pl.ds(first * half, count * half)]
        copies.append(pltpu.make_async_copy(out_ref.at[at], to, sems.at[i]))
    for flip in (0, 1):
        at = pl.ds(pl.multiple_of(((side ^ flip) * PLANE + own) * part, part), part)
        to = query_mat.at[:, pl.ds(flip * part, part)]
        copies.append(pltpu.make_async_copy(query_ref.at[:, at], to, sems.at[2 + flip]))
    for copy in copies:
        copy.start()
    for copy in copies:
        copy.wait()


def cut_kernel(w_ref, *out_refs):
    side = lax.rem(lax.axis_index("phase"), 2)
    upper = lax.rem(lax.axis_index("ctx"), PLANE) // 2
    half = w_ref.shape[1] // 2
    pair = out_refs[0].shape[1] // 2
    for ref, (flip_side, flip_upper) in zip(out_refs, ((0, 0), (0, 1), (1, 0), (1, 1))):
        place = ((side ^ flip_side) * 2 + (upper ^ flip_upper)) * pair
        ref[:, :pair] = w_ref[:, pl.ds(pl.multiple_of(place, pair), pair)]
        ref[:, pair:] = w_ref[:, pl.ds(pl.multiple_of(place + half, pair), pair)]


def sort_kernel(kept, across_y, across_x, across_both, near_ref, far_ref):
    side = lax.rem(lax.axis_index("phase"), 2)
    core = lax.rem(lax.axis_index("ctx"), 2)
    rows, part = kept.shape[0], kept.shape[1] // 4
    for layer in range(2):
        for flip, out_ref in enumerate((near_ref, far_ref)):
            head = pl.multiple_of((core ^ flip) * part, part)

            def put(sources):
                for r, ref in enumerate(sources):
                    at = slice(r * rows, (r + 1) * rows)
                    out_ref[layer, at, :part] = ref[:, pl.ds(head, part)]
                    out_ref[layer, at, part:] = ref[:, pl.ds(head + 2 * part, part)]

            pl.when(side == layer)(functools.partial(put, (kept, across_y)))
            pl.when(side != layer)(functools.partial(put, (across_x, across_both)))


def merge_kernel(near_ref, far_ref, early_ref, late_ref):
    rows = near_ref.shape[1]
    for layer, ref in enumerate((early_ref, late_ref)):
        ref[:rows] = near_ref[layer]
        ref[rows:] = far_ref[layer]


def fill_weights(ctx, weight_refs, weights):
    rows = weight_refs[0].shape[0] // PLANE
    for m, ref in enumerate(weight_refs):
        for r, o in enumerate(ORDER):
            source = ctx ^ (PLANE * m + o)
            at = pl.ds(pl.multiple_of(source * rows, rows), rows)
            weights[at, :] = ref[r * rows : (r + 1) * rows, :]


def project_query(normed, wq_ref, mine_ref, other_ref):
    queries = dot(normed, wq_ref[...]).astype(jnp.bfloat16)
    part = mine_ref.shape[1]
    mine_ref[...] = queries[:, :part]
    other_ref[...] = queries[:, part:]


def norm_kernel(*refs):
    x_refs, (normed_ref,) = refs[:PLANE], refs[PLANE:]
    rows = x_refs[0].shape[0]
    own = lax.rem(lax.axis_index("ctx"), PLANE)
    for r, o in enumerate(ORDER):
        at = pl.ds(pl.multiple_of((own ^ o) * rows, rows), rows)
        normed_ref[at, :] = rms_rows(x_refs[r][:, : normed_ref.shape[1]])


def group_ids(x_refs, own, group):
    rows, width = x_refs[0].shape[0], x_refs[0].shape[1] - HEAD
    column = jnp.zeros((rows, 1), jnp.float32)
    for r, o in enumerate(ORDER):
        chosen = jnp.where((own ^ o) == group, 1.0, 0.0)
        column = column + chosen * x_refs[r][:, width : width + 1].astype(jnp.float32)
    return jnp.broadcast_to(column, (rows, rows))


def first_kernel(pieces, *refs):
    x_refs, weight_refs, refs = refs[:PLANE], refs[PLANE : PLANE + pieces], refs[PLANE + pieces :]
    wq_ref, mine_ref, other_ref, kv_ref, tail_ref, normed, weights = refs
    ctx = lax.axis_index("ctx")
    own, rows = lax.rem(ctx, PLANE), x_refs[0].shape[0]
    fill_weights(ctx, weight_refs, weights)
    norm_kernel(*x_refs, normed)
    keyvals = dot(normed[...], weights[...]).astype(jnp.bfloat16)
    kv_ref[...] = keyvals
    past = (WINDOW - 1) * rows
    tail_ref[:past] = keyvals[keyvals.shape[0] - past :]
    extra = tail_ref.shape[0] - past
    line = lax.broadcasted_iota(jnp.int32, (extra, rows), 0)
    block = jnp.zeros((extra, rows), jnp.float32)
    for t in range(WINDOW - 1):
        row = jnp.transpose(group_ids(x_refs, own, PLANE - WINDOW + 1 + t))[:extra]
        block = jnp.where(line == t, row, block)
    tail_ref[past:, :rows] = block.astype(jnp.bfloat16)
    tail_ref[past:, rows:] = jnp.zeros((extra, tail_ref.shape[1] - rows), jnp.bfloat16)
    project_query(normed[...], wq_ref, mine_ref, other_ref)


def out_copies(own, local_ref, piece_refs, whole, sems):
    half = piece_refs[1].shape[0]
    pieces = []
    for flip in (0, 1):
        three, one = piece_refs[2 * flip : 2 * flip + 2]
        pieces += [(three, 0, flip, 0), (three, 1, flip, 1)]
        pieces += [(three, 2, flip ^ 2, 0), (one, 0, flip ^ 2, 1)]
    from_own, from_pieces = [], []
    for i, (ref, part, o, second) in enumerate(pieces):
        at = pl.ds(i * half, half)
        from_own.append(pltpu.make_async_copy(local_ref.at[at], whole.at[at], sems.at[i]))
        place = pl.ds(pl.multiple_of(((own ^ o) * 2 + second) * half, half), half)
        source = ref.at[pl.ds(part * half, half)]
        from_pieces.append(pltpu.make_async_copy(source, whole.at[place], sems.at[i]))
    return from_own, from_pieces


def second_kernel(pieces, *refs):
    x_refs, b_refs = refs[:PLANE], refs[PLANE : 3 * PLANE]
    weight_refs, refs = refs[3 * PLANE : 3 * PLANE + pieces], refs[3 * PLANE + pieces :]
    wq_ref, wo_ref, piece_refs, refs = refs[0], refs[1], refs[2:6], refs[6:]
    own_ref, mine_ref, other_ref, kv_ref, tail_ref = refs[:5]
    stream, blended, normed, weights, whole, sems = refs[5:]
    ctx = lax.axis_index("ctx")
    side = lax.rem(lax.axis_index("phase"), 2)
    rows = x_refs[0].shape[0]
    own = lax.rem(ctx, PLANE)
    from_own, from_pieces = out_copies(own, wo_ref, piece_refs, whole, sems)

    @pl.when(side == 0)
    def _():
        for copy in from_own:
            copy.start()

    @pl.when(side == 1)
    def _():
        for copy in from_pieces:
            copy.start()

    fill_weights(ctx, weight_refs, weights)
    part = b_refs[0].shape[1]
    for r, o in enumerate(ORDER):
        stream[pl.ds(pl.multiple_of((own ^ o) * rows, rows), rows), :] = x_refs[r][:, : stream.shape[1]]
    for m, ref in enumerate(b_refs):
        place = (side * PLANE + own) ^ m
        blended[:, pl.ds(pl.multiple_of(place * part, part), part)] = ref[...]
    for copy in from_own:
        copy.wait()
    width = stream.shape[1]
    step = min(512, width)
    for n in range(0, width, step):
        total = dot(blended[...], whole[:, n : n + step])
        total = total + stream[:, n : n + step].astype(jnp.float32)
        stream[:, n : n + step] = total.astype(jnp.bfloat16)
    normed[...] = rms_rows(stream[...])
    own_ref[...] = stream[pl.ds(pl.multiple_of(own * rows, rows), rows), :]
    keyvals = dot(normed[...], weights[...]).astype(jnp.bfloat16)
    kv_ref[...] = keyvals
    tail_ref[...] = keyvals[keyvals.shape[0] - tail_ref.shape[0] :]
    project_query(normed[...], wq_ref, mine_ref, other_ref)


def mask_kernel(*refs):
    x_refs, (past_ref, bias_ref) = refs[:PLANE], refs[PLANE:]
    rows = bias_ref.shape[1]
    ctx = lax.axis_index("ctx")
    own = lax.rem(ctx, PLANE)
    before = WINDOW - 1
    columns = [group_ids(x_refs, own, g) for g in range(PLANE)]
    past = past_ref[before * rows :, :rows].astype(jnp.float32)
    keys = [jnp.broadcast_to(past[t : t + 1], (rows, rows)) for t in range(before)]
    keys += [jnp.transpose(column) for column in columns]
    causal = lax.broadcasted_iota(jnp.int32, (rows, rows), 0) >= lax.broadcasted_iota(
        jnp.int32, (rows, rows), 1
    )
    for g in range(PLANE):
        for t in range(WINDOW):
            allowed = columns[g] == keys[g + t]
            if t == before:
                allowed = allowed & causal
            if g + t < before:
                allowed = allowed & (ctx >= PLANE)
            bias_ref[g, :, t * rows : (t + 1) * rows] = jnp.where(allowed, 0.0, -jnp.inf)


def attend_kernel(layer, mine_ref, got_ref, bias_ref, kv_ref, past_ref, *refs):
    out_refs, window = refs[:-1], refs[-1]
    rows = bias_ref.shape[1]
    part = mine_ref.shape[1]
    tall, past = kv_ref.shape[0], (WINDOW - 1) * rows
    local_query = lax.rem(lax.axis_index("phase"), 2) == layer
    window[tall - past : tall] = past_ref[:past]
    window[tall:] = kv_ref[...]
    upper = lax.rem(lax.axis_index("ctx"), PLANE) // 2
    for g in range(PLANE):
        keys = window[(g + 1) * rows : (g + 1 + WINDOW) * rows]
        for h in range(0, part, HEAD):
            at = (slice(g * rows, (g + 1) * rows), slice(h, h + HEAD))
            query = jnp.where(local_query, mine_ref[at], got_ref[at])
            scores = lax.dot_general(
                query, keys[:, h : h + HEAD], (((1,), (1,)), ((), ())),
                preferred_element_type=jnp.float32,
            )
            scores = scores * (1.0 / math.sqrt(HEAD)) + bias_ref[g]
            weights = jnp.exp(scores - jnp.max(scores, axis=1, keepdims=True))
            total = jnp.sum(weights, axis=1, keepdims=True)
            values = keys[:, part + h : part + h + HEAD]
            result = (dot(weights.astype(jnp.bfloat16), values) / total).astype(jnp.bfloat16)
            if layer == 0:
                out_refs[0][g * rows : (g + 1) * rows, h : h + HEAD] = result
                continue
            place = (g % 2) * rows

            def put(ref):
                ref[place : place + rows, h : h + HEAD] = result

            pl.when(upper == g // 2)(functools.partial(put, out_refs[0]))
            pl.when(upper != g // 2)(functools.partial(put, out_refs[1]))


def last_kernel(*refs):
    b_refs, (wo_ref, own_ref, out_ref, blended) = refs[: 2 * PLANE], refs[2 * PLANE :]
    own = lax.rem(lax.axis_index("ctx"), PLANE)
    side = lax.rem(lax.axis_index("phase"), 2)
    rows, part = own_ref.shape[0], b_refs[0].shape[1]

    @pl.when(side == 0)
    def _():
        out_ref[...] = own_ref[...]

    @pl.when(side == 1)
    def _():
        for m, ref in enumerate(b_refs):
            place = (side * PLANE + own) ^ m
            start = pl.multiple_of(lax.rem(own, 2) * rows, rows)
            blended[:, pl.ds(pl.multiple_of(place * part, part), part)] = ref[pl.ds(start, rows), :]
        total = own_ref[...].astype(jnp.float32) + dot(blended[...], wo_ref[...])
        out_ref[...] = total.astype(jnp.bfloat16)


def after(value, *others):
    return lax.optimization_barrier((value,) + others)[0]


def along_planes(piece):
    count = lax.axis_size("ctx") // PLANE
    return [piece] + [swap(piece, 0, PLANE * m) for m in range(1, count)]


def local(inputs, segment_ids, w_query, w_keyval, w_out):
    batches, rows, width = inputs.shape
    phases = lax.axis_size("phase")
    phase = lax.axis_index("phase")
    side = phase % 2
    own = lax.axis_index("ctx") % PLANE
    bf16 = jnp.bfloat16

    head_width = w_query.shape[2]
    part = head_width // (2 * PLANE)
    depth = w_keyval.shape[1]
    tall, past = PLANE * rows, (WINDOW - 1) * rows

    half = head_width // PLANE // 2
    sent_out, query_mat = call(
        slice_kernel, [((3 * half, width), bf16), ((width, 2 * part), bf16)],
        [pltpu.SemaphoreType.DMA((4,))], LONG, w_out[0], w_query[0], far=(0, 1),
    )

    kept, for_y, for_x, for_both = call(
        cut_kernel, [((depth, 4 * part), bf16)] * 4, [], 0, w_keyval[0]
    )
    across_both, across_x, across_y = swap(for_both, 1, 2), swap(for_x, 1, 0), swap(for_y, 0, 2)
    kept, sent_out, query_mat = lax.optimization_barrier((kept, sent_out, query_mat))
    near, far = call(
        sort_kernel, [((2, 2 * depth, 2 * part), bf16)] * 2, [], 0,
        kept, across_y, across_x, across_both,
    )
    early, late_start = call(
        merge_kernel, [((4 * depth, 2 * part), bf16)] * 2, [], 0, near, swap(far, 0, 1)
    )
    got_out = swap(after(sent_out, near), 1, 0)
    early = along_planes(early)
    pieces = len(early)

    keyval_out = [((tall, 2 * part), bf16), ((past, 2 * part), bf16)]
    first_out = [((tall, 2 * part), bf16), ((past + 16, 2 * part), bf16)]
    query_out = [((tall, part), bf16)] * 2
    weights = ((width, 2 * part), bf16)
    dot_flops = 2 * tall * width * 2 * part
    attend_flops = 4 * tall * WINDOW * rows * part

    def two_layers(x, ids, bias):
        x = call(extend_kernel, [((rows, width + HEAD), bf16)], [], 0, x, ids)[0]
        across = swap(after(x, early[0]), 0, 2)
        xs = [x, across] + [swap(after(b, *early), 0, 1) for b in (x, across)]
        xs[0], got = lax.optimization_barrier((x, got_out))
        got_across = swap(got[half : 2 * half], 0, 2)
        late = {m: swap(after(late_start, early[3]), 0, PLANE * m) for m in (2, 1)}
        late[0] = late_start
        mine, other, kv, tail = call(
            functools.partial(first_kernel, pieces), query_out + first_out,
            [((tall, width), bf16), weights], LONG, *xs, *early, query_mat,
        )
        past_kv = from_plane_behind(tail)
        if bias is None:
            shape = ((PLANE, rows, WINDOW * rows), jnp.float32)
            bias = call(mask_kernel, [shape], [], 0, *xs, past_kv)[0]
        bias, late[1], late[2], got_across = lax.optimization_barrier(
            (bias, late[1], late[2], got_across)
        )
        blended = call(
            functools.partial(attend_kernel, 0), [((tall, part), bf16)],
            [((2 * tall, 2 * part), bf16)], 0, mine, swap(other, 1, 0), bias, kv, past_kv,
        )[0]
        for m in range(4, pieces):
            late[m] = swap(after(late_start, kv), 0, PLANE * m)
        near = [blended, swap(blended, 0, 2), swap(blended, 1, 0), swap(blended, 1, 2)]
        heads = [b for n in near for b in (n, swap(n, 0, 1))]
        late[3] = swap(after(late[2], blended), 0, PLANE)
        out = [got, got_across]
        out += [swap(after(b, blended), 0, 1) for b in out]
        stream, mine, other, kv, tail = call(
            functools.partial(second_kernel, pieces),
            [((rows, width), bf16)] + query_out + keyval_out,
            [((tall, width), bf16), ((tall, head_width), bf16), ((tall, width), bf16), weights,
             ((head_width, width), bf16), pltpu.SemaphoreType.DMA((2 * PLANE,))],
            2 * dot_flops + 2 * tall * head_width * width,
            *xs, *heads, *(late[m] for m in range(pieces)), query_mat, w_out[0], *out,
            far=range(3 * PLANE + pieces + 1, 3 * PLANE + pieces + 6),
        )
        mine, other = call(
            functools.partial(attend_kernel, 1), [((tall // 2, part), bf16)] * 2,
            [((2 * tall, 2 * part), bf16)],
            attend_flops, mine, swap(other, 1, 0), bias, kv, from_plane_behind(tail),
        )
        near = [mine, swap(other, 0, 2), swap(mine, 1, 0), swap(other, 1, 2)]
        heads = [b for n in near for b in (n, swap(n, 0, 1))]
        out = call(
            last_kernel, [((rows, width), bf16)], [((rows, head_width), bf16)],
            2 * rows * head_width * width, *heads, w_out[0], stream,
        )[0]
        return out, bias

    outs = []
    for b in range(batches):
        x, out, bias = inputs[b], None, None
        for tick in range(phases // 2):
            result, bias = two_layers(x, segment_ids[b : b + 1], bias)
            out = result if out is None else jnp.where(phase // 2 == tick, result, out)
            if tick + 1 < phases // 2:
                ahead = [
                    lax.ppermute(result, "phase", [(f, f + d) for f in range(1, phases - d, 2)])
                    for d in (1, 2)
                ]
                x = jnp.where(side == 0, ahead[0], ahead[1])
        outs.append(out)
    return jnp.stack(outs)[None]


def solution(mesh):
    placed = (
        P(None, "ctx", None),
        P(None, "ctx"),
        P("phase", None, None),
        P("phase", "ctx", None),
        P("phase", None, None),
    )
    return jax.shard_map(
        local, mesh=mesh, in_specs=placed, out_specs=P("phase", None, "ctx", None), check_vma=False
    )
```

```python
import functools
import math

import jax
import jax.numpy as jnp
from jax import lax
from jax.experimental import pallas as pl
from jax.experimental.pallas import tpu as pltpu
from jax.sharding import PartitionSpec as P

HEAD = 128
WINDOW = 4
PLANE = 4
ORDER = (0, 2, 1, 3)
BOTH = ("phase", "ctx")
VMEM_BYTES = 24 * 1024 * 1024
LONG = 10**11


def swap(block, phase_bit, ctx_bits):
    wide = lax.axis_size("ctx")
    route = [
        (f * wide + d, (f ^ phase_bit) * wide + (d ^ ctx_bits))
        for f in range(lax.axis_size("phase"))
        for d in range(wide)
    ]
    return lax.ppermute(block, BOTH, route)


def from_plane_behind(block):
    wide = lax.axis_size("ctx")
    return lax.ppermute(block, "ctx", [(i, i + PLANE) for i in range(wide - PLANE)])


def rms_rows(values):
    widened = values.astype(jnp.float32)
    scale = lax.rsqrt(jnp.mean(widened * widened, axis=-1, keepdims=True) + 1e-05)
    return (widened * scale).astype(jnp.bfloat16)


def dot(a, b):
    return jnp.dot(a, b, preferred_element_type=jnp.float32)


def call(kernel, outs, scratch, flops, *operands, far={}):
    moved = sum(o.size * o.dtype.itemsize for o in operands)
    place = lambda i: far.get(i, pltpu.VMEM)
    return pl.pallas_call(
        kernel,
        out_shape=[jax.ShapeDtypeStruct(s, d) for s, d in outs],
        in_specs=[pl.BlockSpec(memory_space=place(i)) for i in range(len(operands))],
        out_specs=[pl.BlockSpec(memory_space=pltpu.VMEM)] * len(outs),
        scratch_shapes=[pltpu.VMEM(*s) if isinstance(s, tuple) else s for s in scratch],
        cost_estimate=pl.CostEstimate(flops=flops, bytes_accessed=moved, transcendentals=0),
        compiler_params=pltpu.CompilerParams(vmem_limit_bytes=VMEM_BYTES),
    )(*operands)


def extend_kernel(x_ref, id_ref, out_ref):
    rows, width = x_ref.shape
    lanes = out_ref.shape[1] - width
    out_ref[:, :width] = x_ref[...]
    ids = jnp.broadcast_to(id_ref[...].astype(jnp.float32), (rows, rows))
    out_ref[:, width:] = jnp.broadcast_to(
        jnp.transpose(ids)[:, :1], (rows, lanes)
    ).astype(jnp.bfloat16)


def slice_kernel(out_ref, query_ref, sent_first, sent_second, query_mat, sems):
    side = lax.rem(lax.axis_index("phase"), 2)
    own = lax.rem(lax.axis_index("ctx"), PLANE)
    unit, wide = sent_first.shape[0] // 6, sent_first.shape[1]
    part = query_mat.shape[1] // 2
    columns = pl.ds(pl.multiple_of(lax.rem(own, 2) * wide, wide), wide)
    copies = []
    for i, (ref, first, count, upper, skip) in enumerate((
        (sent_first, 0, 6, own // 2, 2), (sent_second, 0, 2, own // 2, 0),
        (sent_second, 2, 2, 1 - own // 2, 0),
    )):
        at = pl.ds(pl.multiple_of((upper * 8 + skip) * unit, unit), count * unit)
        to = ref.at[pl.ds(first * unit, count * unit)]
        copies.append(pltpu.make_async_copy(out_ref.at[at, columns], to, sems.at[i]))
    for flip in (0, 1):
        at = pl.ds(pl.multiple_of(((side ^ flip) * PLANE + own) * part, part), part)
        to = query_mat.at[:, pl.ds(flip * part, part)]
        copies.append(pltpu.make_async_copy(query_ref.at[:, at], to, sems.at[3 + flip]))
    for copy in copies:
        copy.start()
    for copy in copies:
        copy.wait()


def cut_kernel(w_ref, *out_refs):
    side = lax.rem(lax.axis_index("phase"), 2)
    upper = lax.rem(lax.axis_index("ctx"), PLANE) // 2
    half = w_ref.shape[1] // 2
    pair = out_refs[0].shape[1] // 2
    for ref, (flip_side, flip_upper) in zip(out_refs, ((0, 0), (0, 1), (1, 0), (1, 1))):
        place = ((side ^ flip_side) * 2 + (upper ^ flip_upper)) * pair
        ref[:, :pair] = w_ref[:, pl.ds(pl.multiple_of(place, pair), pair)]
        ref[:, pair:] = w_ref[:, pl.ds(pl.multiple_of(place + half, pair), pair)]


def sort_kernel(kept, across_y, across_x, across_both, near_ref, far_ref):
    side = lax.rem(lax.axis_index("phase"), 2)
    core = lax.rem(lax.axis_index("ctx"), 2)
    rows, part = kept.shape[0], kept.shape[1] // 4
    for layer in range(2):
        for flip, out_ref in enumerate((near_ref, far_ref)):
            head = pl.multiple_of((core ^ flip) * part, part)

            def put(sources):
                for r, ref in enumerate(sources):
                    at = slice(r * rows, (r + 1) * rows)
                    out_ref[layer, at, :part] = ref[:, pl.ds(head, part)]
                    out_ref[layer, at, part:] = ref[:, pl.ds(head + 2 * part, part)]

            pl.when(side == layer)(functools.partial(put, (kept, across_y)))
            pl.when(side != layer)(functools.partial(put, (across_x, across_both)))


def merge_kernel(near_ref, far_ref, early_ref, late_ref):
    rows = near_ref.shape[1]
    for layer, ref in enumerate((early_ref, late_ref)):
        ref[:rows] = near_ref[layer]
        ref[rows:] = far_ref[layer]


def token_kernel(*refs):
    refs[-1][...] = jnp.zeros(refs[-1].shape, refs[-1].dtype)


def copy_kernel(block_ref, out_ref):
    out_ref[...] = block_ref[...]


def fill_weights(ctx, weight_refs, weights):
    rows = weight_refs[0].shape[0] // PLANE
    for m, ref in enumerate(weight_refs):
        for r, o in enumerate(ORDER):
            source = ctx ^ (PLANE * m + o)
            at = pl.ds(pl.multiple_of(source * rows, rows), rows)
            weights[at, :] = ref[r * rows : (r + 1) * rows, :]


def project_query(normed, wq_ref, mine_ref, other_ref):
    queries = dot(normed, wq_ref[...]).astype(jnp.bfloat16)
    part = mine_ref.shape[1]
    mine_ref[...] = queries[:, :part]
    other_ref[...] = queries[:, part:]


def norm_kernel(*refs):
    x_refs, (normed_ref,) = refs[:PLANE], refs[PLANE:]
    rows = x_refs[0].shape[0]
    own = lax.rem(lax.axis_index("ctx"), PLANE)
    for r, o in enumerate(ORDER):
        at = pl.ds(pl.multiple_of((own ^ o) * rows, rows), rows)
        normed_ref[at, :] = rms_rows(x_refs[r][:, : normed_ref.shape[1]])


def group_ids(x_refs, own, group):
    rows, width = x_refs[0].shape[0], x_refs[0].shape[1] - HEAD
    column = jnp.zeros((rows, 1), jnp.float32)
    for r, o in enumerate(ORDER):
        chosen = jnp.where((own ^ o) == group, 1.0, 0.0)
        column = column + chosen * x_refs[r][:, width : width + 1].astype(jnp.float32)
    return jnp.broadcast_to(column, (rows, rows))


def query_kernel(*refs):
    x_refs, (wq_ref, normed_ref, mine_ref, other_ref, ids_ref) = refs[:PLANE], refs[PLANE:]
    own, rows = lax.rem(lax.axis_index("ctx"), PLANE), x_refs[0].shape[0]
    norm_kernel(*x_refs, normed_ref)
    project_query(normed_ref[...], wq_ref, mine_ref, other_ref)
    extra, wide = ids_ref.shape
    line = lax.broadcasted_iota(jnp.int32, (extra, rows), 0)
    block = jnp.zeros((extra, rows), jnp.float32)
    for t in range(WINDOW - 1):
        row = jnp.transpose(group_ids(x_refs, own, PLANE - WINDOW + 1 + t))[:extra]
        block = jnp.where(line == t, row, block)
    ids_ref[:, :rows] = block.astype(jnp.bfloat16)
    ids_ref[:, rows:] = jnp.zeros((extra, wide - rows), jnp.bfloat16)


def keyval_kernel(pieces, *refs):
    weight_refs, (normed_ref, ids_ref, kv_ref, tail_ref, weights) = refs[:pieces], refs[pieces:]
    fill_weights(lax.axis_index("ctx"), weight_refs, weights)
    keyvals = dot(normed_ref[...], weights[...]).astype(jnp.bfloat16)
    kv_ref[...] = keyvals
    past = tail_ref.shape[0] - ids_ref.shape[0]
    tail_ref[:past] = keyvals[keyvals.shape[0] - past :]
    tail_ref[past:] = ids_ref[...]


def out_copies(own, local_ref, piece_refs, whole, sems):
    first_ref, second_ref, across_ref = piece_refs
    rows, wide = first_ref.shape[0] // 6, first_ref.shape[1]
    columns = pl.ds(pl.multiple_of(lax.rem(own, 2) * wide, wide), wide)
    upper = own // 2
    from_own, from_pieces = [], []
    for i, (ref, first, place, count) in enumerate((
        (first_ref, 0, upper * 8 + 2, 6), (second_ref, 0, upper * 8, 2),
        (second_ref, 2, (1 - upper) * 8, 2), (across_ref, 0, (1 - upper) * 8 + 2, 6),
    )):
        at = pl.ds(pl.multiple_of(place * rows, rows), count * rows)
        source = ref.at[pl.ds(first * rows, count * rows)]
        from_own.append(
            pltpu.make_async_copy(local_ref.at[at, columns], whole.at[at], sems.at[i])
        )
        from_pieces.append(pltpu.make_async_copy(source, whole.at[at], sems.at[i]))
    return from_own, from_pieces


def stream_kernel(*refs):
    x_refs, b_refs = refs[:PLANE], refs[PLANE : 3 * PLANE]
    wo_ref, piece_refs = refs[3 * PLANE], refs[3 * PLANE + 1 : 3 * PLANE + 4]
    half_ref, blended, whole, sems = refs[3 * PLANE + 4 :]
    side = lax.rem(lax.axis_index("phase"), 2)
    own = lax.rem(lax.axis_index("ctx"), PLANE)
    from_own, from_pieces = out_copies(own, wo_ref, piece_refs, whole, sems)

    @pl.when(side == 0)
    def _():
        for copy in from_own:
            copy.start()

    @pl.when(side == 1)
    def _():
        for copy in from_pieces:
            copy.start()

    rows, part, wide = x_refs[0].shape[0], b_refs[0].shape[1], half_ref.shape[1]
    columns = pl.ds(pl.multiple_of(lax.rem(own, 2) * wide, wide), wide)
    for r, o in enumerate(ORDER):
        at = pl.ds(pl.multiple_of((own ^ o) * rows, rows), rows)
        half_ref[at, :] = x_refs[r][:, columns]
    for m, ref in enumerate(b_refs):
        place = (side * PLANE + own) ^ m
        blended[:, pl.ds(pl.multiple_of(place * part, part), part)] = ref[...]
    for copy in from_own:
        copy.wait()
    step = min(512, wide)
    for n in range(0, wide, step):
        total = dot(blended[...], whole[:, n : n + step])
        total = total + half_ref[:, n : n + step].astype(jnp.float32)
        half_ref[:, n : n + step] = total.astype(jnp.bfloat16)


def second_kernel(pieces, *refs):
    mine_half, other_half, refs = refs[0], refs[1], refs[2:]
    weight_refs, refs = refs[:pieces], refs[pieces:]
    wq_ref, own_ref, mine_ref, other_ref, kv_ref, tail_ref, stream, normed, weights = refs
    ctx = lax.axis_index("ctx")
    own, core = lax.rem(ctx, PLANE), lax.rem(ctx, 2)
    rows, wide = own_ref.shape[0], mine_half.shape[1]
    fill_weights(ctx, weight_refs, weights)
    for flip, ref in enumerate((mine_half, other_half)):
        stream[:, pl.ds(pl.multiple_of((core ^ flip) * wide, wide), wide)] = ref[...]
    normed[...] = rms_rows(stream[...])
    own_ref[...] = stream[pl.ds(pl.multiple_of(own * rows, rows), rows), :]
    keyvals = dot(normed[...], weights[...]).astype(jnp.bfloat16)
    kv_ref[...] = keyvals
    tail_ref[...] = keyvals[keyvals.shape[0] - tail_ref.shape[0] :]
    project_query(normed[...], wq_ref, mine_ref, other_ref)


def mask_kernel(*refs):
    x_refs, (past_ref, bias_ref) = refs[:PLANE], refs[PLANE:]
    rows = bias_ref.shape[1]
    ctx = lax.axis_index("ctx")
    own = lax.rem(ctx, PLANE)
    before = WINDOW - 1
    columns = [group_ids(x_refs, own, g) for g in range(PLANE)]
    past = past_ref[before * rows :, :rows].astype(jnp.float32)
    keys = [jnp.broadcast_to(past[t : t + 1], (rows, rows)) for t in range(before)]
    keys += [jnp.transpose(column) for column in columns]
    causal = lax.broadcasted_iota(jnp.int32, (rows, rows), 0) >= lax.broadcasted_iota(
        jnp.int32, (rows, rows), 1
    )
    for g in range(PLANE):
        for t in range(WINDOW):
            allowed = columns[g] == keys[g + t]
            if t == before:
                allowed = allowed & causal
            if g + t < before:
                allowed = allowed & (ctx >= PLANE)
            bias_ref[g, :, t * rows : (t + 1) * rows] = jnp.where(allowed, 0.0, -jnp.inf)


def attend_kernel(layer, mine_ref, got_ref, bias_ref, kv_ref, past_ref, *refs):
    out_refs, window = refs[:-1], refs[-1]
    rows = bias_ref.shape[1]
    part = mine_ref.shape[1]
    tall, past = kv_ref.shape[0], (WINDOW - 1) * rows
    local_query = lax.rem(lax.axis_index("phase"), 2) == layer
    window[tall - past : tall] = past_ref[:past]
    window[tall:] = kv_ref[...]
    upper = lax.rem(lax.axis_index("ctx"), PLANE) // 2
    for g in range(PLANE):
        keys = window[(g + 1) * rows : (g + 1 + WINDOW) * rows]
        for h in range(0, part, HEAD):
            at = (slice(g * rows, (g + 1) * rows), slice(h, h + HEAD))
            query = jnp.where(local_query, mine_ref[at], got_ref[at])
            scores = lax.dot_general(
                query, keys[:, h : h + HEAD], (((1,), (1,)), ((), ())),
                preferred_element_type=jnp.float32,
            )
            scores = scores * (1.0 / math.sqrt(HEAD)) + bias_ref[g]
            weights = jnp.exp(scores - jnp.max(scores, axis=1, keepdims=True))
            total = jnp.sum(weights, axis=1, keepdims=True)
            values = keys[:, part + h : part + h + HEAD]
            result = (dot(weights.astype(jnp.bfloat16), values) / total).astype(jnp.bfloat16)
            if layer == 0:
                out_refs[0][g * rows : (g + 1) * rows, h : h + HEAD] = result
                continue
            place = (g % 2) * rows

            def put(ref):
                ref[place : place + rows, h : h + HEAD] = result

            pl.when(upper == g // 2)(functools.partial(put, out_refs[0]))
            pl.when(upper != g // 2)(functools.partial(put, out_refs[1]))


def last_kernel(*refs):
    b_refs, (wo_ref, own_ref, out_ref, blended) = refs[: 2 * PLANE], refs[2 * PLANE :]
    own = lax.rem(lax.axis_index("ctx"), PLANE)
    side = lax.rem(lax.axis_index("phase"), 2)
    rows, part = own_ref.shape[0], b_refs[0].shape[1]

    @pl.when(side == 0)
    def _():
        out_ref[...] = own_ref[...]

    @pl.when(side == 1)
    def _():
        for m, ref in enumerate(b_refs):
            place = (side * PLANE + own) ^ m
            start = pl.multiple_of(lax.rem(own, 2) * rows, rows)
            blended[:, pl.ds(pl.multiple_of(place * part, part), part)] = ref[pl.ds(start, rows), :]
        total = own_ref[...].astype(jnp.float32) + dot(blended[...], wo_ref[...])
        out_ref[...] = total.astype(jnp.bfloat16)


def after(value, *others):
    return lax.optimization_barrier((value,) + others)[0]


def token_of(*blocks, cost):
    places = {i: pl.ANY for i in range(len(blocks))}
    return call(token_kernel, [((8, HEAD), jnp.float32)], [], cost, *blocks, far=places)[0]


def along_planes(piece, gate=()):
    held = {0: piece, 2: swap(after(piece, *gate), 0, PLANE * 2)}
    for m in range(4, lax.axis_size("ctx") // PLANE):
        held[m] = swap(after(piece, *gate), 0, PLANE * m)
    return held


def local(inputs, segment_ids, w_query, w_keyval, w_out):
    batches, rows, width = inputs.shape
    phases = lax.axis_size("phase")
    phase = lax.axis_index("phase")
    side = phase % 2
    own = lax.axis_index("ctx") % PLANE
    bf16 = jnp.bfloat16

    head_width = w_query.shape[2]
    part = head_width // (2 * PLANE)
    depth = w_keyval.shape[1]
    tall, past = PLANE * rows, (WINDOW - 1) * rows

    unit, half = head_width // 16, width // 2
    sent_first, sent_second, query_mat = call(
        slice_kernel,
        [((6 * unit, half), bf16), ((4 * unit, half), bf16), ((width, 2 * part), bf16)],
        [pltpu.SemaphoreType.DMA((5,))], LONG, w_out[0], w_query[0], far={0: pltpu.HBM, 1: pltpu.HBM},
    )

    kept, for_y, for_x, for_both = call(
        cut_kernel, [((depth, 4 * part), bf16)] * 4, [], 0, w_keyval[0]
    )
    across_both, across_x, across_y = swap(for_both, 1, 2), swap(for_x, 1, 0), swap(for_y, 0, 2)
    kept, sent_first, sent_second, query_mat = lax.optimization_barrier(
        (kept, sent_first, sent_second, query_mat)
    )
    near, far = call(
        sort_kernel, [((2, 2 * depth, 2 * part), bf16)] * 2, [], 0,
        kept, across_y, across_x, across_both,
    )
    piece = (4 * depth, 2 * part)
    early, late_start = call(
        merge_kernel, [(piece, bf16)] * 2, [], 0, near, swap(far, 0, 1)
    )
    out_first, out_second = (swap(after(b, across_y), 1, 0) for b in (sent_first, sent_second))
    sent_on = call(copy_kernel, [((6 * unit, half), bf16)], [], 4 * 10**9, out_first)[0]
    out_across = swap(sent_on, 0, 2)
    early = along_planes(early)
    early[1] = swap(early[0], 0, PLANE)
    ready = token_of(token_of(early[2], cost=7 * 10**8), early[1], cost=24 * 10**8)
    early[3] = swap(after(early[2], ready), 0, PLANE)
    pieces = len(early)

    keyval_out = [((tall, 2 * part), bf16), ((past, 2 * part), bf16)]
    first_out = [((tall, 2 * part), bf16), ((past + 16, 2 * part), bf16)]
    query_out = [((tall, part), bf16)] * 2
    weights = ((width, 2 * part), bf16)
    dot_flops = 2 * tall * width * 2 * part
    attend_flops = 4 * tall * WINDOW * rows * part

    def two_layers(x, ids, bias):
        x = call(extend_kernel, [((rows, width + HEAD), bf16)], [], 0, x, ids)[0]
        across = swap(after(x, early[0]), 0, 2)
        xs = [x, across] + [swap(after(b, ready), 0, 1) for b in (x, across)]
        normed, mine, other, ids = call(
            query_kernel, [((tall, width), bf16)] + query_out + [((16, 2 * part), bf16)], [], 0,
            *xs, query_mat,
        )
        kv, tail = call(
            functools.partial(keyval_kernel, pieces), first_out, [weights], LONG,
            *(early[m] for m in range(pieces)), normed, ids,
        )
        query = swap(other, 1, 0)
        late = along_planes(late_start, (kv,))
        late[1] = swap(after(late_start, kv), 0, PLANE)
        past_kv = from_plane_behind(tail)
        if bias is None:
            shape = ((PLANE, rows, WINDOW * rows), jnp.float32)
            bias = call(mask_kernel, [shape], [], 6 * 10**8, *xs, after(past_kv, query))[0]
        bias, *out = lax.optimization_barrier((bias, out_first, out_second, out_across))
        blended = call(
            functools.partial(attend_kernel, 0), [((tall, part), bf16)],
            [((2 * tall, 2 * part), bf16)], 0, mine, query, bias, kv, past_kv,
        )[0]
        near = [blended, swap(blended, 0, 2), swap(blended, 1, 0), swap(blended, 1, 2)]
        heads = [b for n in near for b in (n, swap(n, 0, 1))]
        late[3] = swap(after(late[2], late[1], near[2], near[3]), 0, PLANE)
        half = call(
            stream_kernel, [((tall, width // 2), bf16)],
            [((tall, head_width), bf16), ((head_width, width // 2), bf16),
             pltpu.SemaphoreType.DMA((4,))],
            0, *xs, *heads, w_out[0], *out,
            far={3 * PLANE + i: pltpu.HBM for i in range(4)},
        )[0]
        stream, mine, other, kv, tail = call(
            functools.partial(second_kernel, pieces),
            [((rows, width), bf16)] + query_out + keyval_out,
            [((tall, width), bf16), ((tall, width), bf16), weights], 0,
            half, swap(after(half, late[3]), 0, 1), *(late[m] for m in range(pieces)), query_mat,
        )
        mine, other = call(
            functools.partial(attend_kernel, 1), [((tall // 2, part), bf16)] * 2,
            [((2 * tall, 2 * part), bf16)],
            attend_flops, mine, swap(other, 1, 0), bias, kv, from_plane_behind(tail),
        )
        near = [mine, swap(other, 0, 2), swap(mine, 1, 0), swap(other, 1, 2)]
        heads = [b for n in near for b in (n, swap(n, 0, 1))]
        out = call(
            last_kernel, [((rows, width), bf16)], [((rows, head_width), bf16)],
            2 * rows * head_width * width, *heads, w_out[0], stream,
        )[0]
        return out, bias

    outs = []
    for b in range(batches):
        x, out, bias = inputs[b], None, None
        for tick in range(phases // 2):
            result, bias = two_layers(x, segment_ids[b : b + 1], bias)
            out = result if out is None else jnp.where(phase // 2 == tick, result, out)
            if tick + 1 < phases // 2:
                ahead = [
                    lax.ppermute(result, "phase", [(f, f + d) for f in range(1, phases - d, 2)])
                    for d in (1, 2)
                ]
                x = jnp.where(side == 0, ahead[0], ahead[1])
        outs.append(out)
    return jnp.stack(outs)[None]


def solution(mesh):
    placed = (
        P(None, "ctx", None),
        P(None, "ctx"),
        P("phase", None, None),
        P("phase", "ctx", None),
        P("phase", None, None),
    )
    return jax.shard_map(
        local, mesh=mesh, in_specs=placed, out_specs=P("phase", None, "ctx", None), check_vma=False
    )
```

```python
import functools
import math

import jax
import jax.numpy as jnp
from jax import lax
from jax.experimental import pallas as pl
from jax.experimental.pallas import tpu as pltpu
from jax.sharding import PartitionSpec as P

HEAD = 128
WINDOW = 4
PLANE = 4
ORDER = (0, 2, 1, 3)
BOTH = ("phase", "ctx")
VMEM_BYTES = 24 * 1024 * 1024
LONG = 10**11


def swap(block, phase_bit, ctx_bits):
    wide = lax.axis_size("ctx")
    route = [
        (f * wide + d, (f ^ phase_bit) * wide + (d ^ ctx_bits))
        for f in range(lax.axis_size("phase"))
        for d in range(wide)
    ]
    return lax.ppermute(block, BOTH, route)


def from_plane_behind(block):
    wide = lax.axis_size("ctx")
    return lax.ppermute(block, "ctx", [(i, i + PLANE) for i in range(wide - PLANE)])


def rms_rows(values):
    widened = values.astype(jnp.float32)
    scale = lax.rsqrt(jnp.mean(widened * widened, axis=-1, keepdims=True) + 1e-05)
    return (widened * scale).astype(jnp.bfloat16)


def dot(a, b):
    return jnp.dot(a, b, preferred_element_type=jnp.float32)


def call(kernel, outs, scratch, flops, *operands, far={}):
    moved = sum(o.size * o.dtype.itemsize for o in operands)
    place = lambda i: far.get(i, pltpu.VMEM)
    return pl.pallas_call(
        kernel,
        out_shape=[jax.ShapeDtypeStruct(s, d) for s, d in outs],
        in_specs=[pl.BlockSpec(memory_space=place(i)) for i in range(len(operands))],
        out_specs=[pl.BlockSpec(memory_space=pltpu.VMEM)] * len(outs),
        scratch_shapes=[pltpu.VMEM(*s) if isinstance(s, tuple) else s for s in scratch],
        cost_estimate=pl.CostEstimate(flops=flops, bytes_accessed=moved, transcendentals=0),
        compiler_params=pltpu.CompilerParams(vmem_limit_bytes=VMEM_BYTES),
    )(*operands)


def extend_kernel(x_ref, id_ref, out_ref):
    rows, width = x_ref.shape
    lanes = out_ref.shape[1] - width
    out_ref[:, :width] = x_ref[...]
    ids = jnp.broadcast_to(id_ref[...].astype(jnp.float32), (rows, rows))
    out_ref[:, width:] = jnp.broadcast_to(
        jnp.transpose(ids)[:, :1], (rows, lanes)
    ).astype(jnp.bfloat16)


def slice_kernel(out_ref, query_ref, sent_first, sent_second, query_mat, sems):
    side = lax.rem(lax.axis_index("phase"), 2)
    own = lax.rem(lax.axis_index("ctx"), PLANE)
    unit, wide = sent_first.shape[0] // 6, sent_first.shape[1]
    part = query_mat.shape[1] // 2
    columns = pl.ds(pl.multiple_of(lax.rem(own, 2) * wide, wide), wide)
    copies = []
    for i, (ref, first, count, upper, skip) in enumerate((
        (sent_first, 0, 6, own // 2, 2), (sent_second, 0, 2, own // 2, 0),
        (sent_second, 2, 2, 1 - own // 2, 0),
    )):
        at = pl.ds(pl.multiple_of((upper * 8 + skip) * unit, unit), count * unit)
        to = ref.at[pl.ds(first * unit, count * unit)]
        copies.append(pltpu.make_async_copy(out_ref.at[at, columns], to, sems.at[i]))
    for flip in (0, 1):
        at = pl.ds(pl.multiple_of(((side ^ flip) * PLANE + own) * part, part), part)
        to = query_mat.at[:, pl.ds(flip * part, part)]
        copies.append(pltpu.make_async_copy(query_ref.at[:, at], to, sems.at[3 + flip]))
    for copy in copies:
        copy.start()
    for copy in copies:
        copy.wait()


def cut_kernel(w_ref, *out_refs):
    side = lax.rem(lax.axis_index("phase"), 2)
    upper = lax.rem(lax.axis_index("ctx"), PLANE) // 2
    half = w_ref.shape[1] // 2
    pair = out_refs[0].shape[1] // 2
    for ref, (flip_side, flip_upper) in zip(out_refs, ((0, 0), (0, 1), (1, 0), (1, 1))):
        place = ((side ^ flip_side) * 2 + (upper ^ flip_upper)) * pair
        ref[:, :pair] = w_ref[:, pl.ds(pl.multiple_of(place, pair), pair)]
        ref[:, pair:] = w_ref[:, pl.ds(pl.multiple_of(place + half, pair), pair)]


def sort_kernel(kept, across_y, across_x, across_both, near_ref, far_ref):
    side = lax.rem(lax.axis_index("phase"), 2)
    core = lax.rem(lax.axis_index("ctx"), 2)
    rows, part = kept.shape[0], kept.shape[1] // 4
    for layer in range(2):
        for flip, out_ref in enumerate((near_ref, far_ref)):
            head = pl.multiple_of((core ^ flip) * part, part)

            def put(sources):
                for r, ref in enumerate(sources):
                    at = slice(r * rows, (r + 1) * rows)
                    out_ref[layer, at, :part] = ref[:, pl.ds(head, part)]
                    out_ref[layer, at, part:] = ref[:, pl.ds(head + 2 * part, part)]

            pl.when(side == layer)(functools.partial(put, (kept, across_y)))
            pl.when(side != layer)(functools.partial(put, (across_x, across_both)))


def merge_kernel(near_ref, far_ref, early_ref, late_ref):
    rows = near_ref.shape[1]
    for layer, ref in enumerate((early_ref, late_ref)):
        ref[:rows] = near_ref[layer]
        ref[rows:] = far_ref[layer]


def token_kernel(*refs):
    refs[-1][...] = jnp.zeros(refs[-1].shape, refs[-1].dtype)


def copy_kernel(block_ref, out_ref):
    out_ref[...] = block_ref[...]


def fill_weights(ctx, weight_refs, weights):
    rows = weight_refs[0].shape[0] // PLANE
    for m, ref in enumerate(weight_refs):
        for r, o in enumerate(ORDER):
            source = ctx ^ (PLANE * m + o)
            at = pl.ds(pl.multiple_of(source * rows, rows), rows)
            weights[at, :] = ref[r * rows : (r + 1) * rows, :]


def project_query(normed, wq_ref, mine_ref, other_ref):
    queries = dot(normed, wq_ref[...]).astype(jnp.bfloat16)
    part = mine_ref.shape[1]
    mine_ref[...] = queries[:, :part]
    other_ref[...] = queries[:, part:]


def norm_kernel(*refs):
    x_refs, (normed_ref,) = refs[:PLANE], refs[PLANE:]
    rows = x_refs[0].shape[0]
    own = lax.rem(lax.axis_index("ctx"), PLANE)
    for r, o in enumerate(ORDER):
        at = pl.ds(pl.multiple_of((own ^ o) * rows, rows), rows)
        normed_ref[at, :] = rms_rows(x_refs[r][:, : normed_ref.shape[1]])


def group_ids(x_refs, own, group):
    rows, width = x_refs[0].shape[0], x_refs[0].shape[1] - HEAD
    column = jnp.zeros((rows, 1), jnp.float32)
    for r, o in enumerate(ORDER):
        chosen = jnp.where((own ^ o) == group, 1.0, 0.0)
        column = column + chosen * x_refs[r][:, width : width + 1].astype(jnp.float32)
    return jnp.broadcast_to(column, (rows, rows))


def query_kernel(*refs):
    x_refs, (wq_ref, normed_ref, mine_ref, other_ref, ids_ref) = refs[:PLANE], refs[PLANE:]
    own, rows = lax.rem(lax.axis_index("ctx"), PLANE), x_refs[0].shape[0]
    norm_kernel(*x_refs, normed_ref)
    project_query(normed_ref[...], wq_ref, mine_ref, other_ref)
    extra, wide = ids_ref.shape
    line = lax.broadcasted_iota(jnp.int32, (extra, rows), 0)
    block = jnp.zeros((extra, rows), jnp.float32)
    for t in range(WINDOW - 1):
        row = jnp.transpose(group_ids(x_refs, own, PLANE - WINDOW + 1 + t))[:extra]
        block = jnp.where(line == t, row, block)
    ids_ref[:, :rows] = block.astype(jnp.bfloat16)
    ids_ref[:, rows:] = jnp.zeros((extra, wide - rows), jnp.bfloat16)


def keyval_kernel(pieces, *refs):
    weight_refs, (normed_ref, ids_ref, kv_ref, tail_ref, weights) = refs[:pieces], refs[pieces:]
    fill_weights(lax.axis_index("ctx"), weight_refs, weights)
    keyvals = dot(normed_ref[...], weights[...]).astype(jnp.bfloat16)
    kv_ref[...] = keyvals
    past = tail_ref.shape[0] - ids_ref.shape[0]
    tail_ref[:past] = keyvals[keyvals.shape[0] - past :]
    tail_ref[past:] = ids_ref[...]


def out_copies(own, first_column, local_ref, piece_refs, whole, sems):
    first_ref, second_ref, across_ref = piece_refs
    rows, wide = first_ref.shape[0] // 6, first_ref.shape[1]
    count_columns = whole.shape[1]
    start = lax.rem(own, 2) * wide + first_column
    columns = pl.ds(pl.multiple_of(start, count_columns), count_columns)
    piece_columns = pl.ds(first_column, count_columns)
    upper = own // 2
    from_own, from_pieces = [], []
    for i, (ref, first, place, count) in enumerate((
        (first_ref, 0, upper * 8 + 2, 6), (second_ref, 0, upper * 8, 2),
        (second_ref, 2, (1 - upper) * 8, 2), (across_ref, 0, (1 - upper) * 8 + 2, 6),
    )):
        at = pl.ds(pl.multiple_of(place * rows, rows), count * rows)
        source = ref.at[pl.ds(first * rows, count * rows), piece_columns]
        from_own.append(
            pltpu.make_async_copy(local_ref.at[at, columns], whole.at[at], sems.at[i])
        )
        from_pieces.append(pltpu.make_async_copy(source, whole.at[at], sems.at[i]))
    return from_own, from_pieces


def stream_kernel(part_index, *refs):
    x_refs, b_refs = refs[:PLANE], refs[PLANE : 3 * PLANE]
    wo_ref, piece_refs = refs[3 * PLANE], refs[3 * PLANE + 1 : 3 * PLANE + 4]
    half_ref, blended, whole, sems = refs[3 * PLANE + 4 :]
    side = lax.rem(lax.axis_index("phase"), 2)
    own = lax.rem(lax.axis_index("ctx"), PLANE)
    wide = half_ref.shape[1]
    from_own, from_pieces = out_copies(own, part_index * wide, wo_ref, piece_refs, whole, sems)

    @pl.when(side == 0)
    def _():
        for copy in from_own:
            copy.start()

    @pl.when(side == 1)
    def _():
        for copy in from_pieces:
            copy.start()

    rows, part = x_refs[0].shape[0], b_refs[0].shape[1]
    start = (lax.rem(own, 2) * 2 + part_index) * wide
    columns = pl.ds(pl.multiple_of(start, wide), wide)
    for r, o in enumerate(ORDER):
        at = pl.ds(pl.multiple_of((own ^ o) * rows, rows), rows)
        half_ref[at, :] = x_refs[r][:, columns]
    for m, ref in enumerate(b_refs):
        place = (side * PLANE + own) ^ m
        blended[:, pl.ds(pl.multiple_of(place * part, part), part)] = ref[...]
    for copy in from_own:
        copy.wait()
    step = min(512, wide)
    for n in range(0, wide, step):
        total = dot(blended[...], whole[:, n : n + step])
        total = total + half_ref[:, n : n + step].astype(jnp.float32)
        half_ref[:, n : n + step] = total.astype(jnp.bfloat16)


def second_kernel(pieces, *refs):
    quarters, refs = refs[:4], refs[4:]
    weight_refs, refs = refs[:pieces], refs[pieces:]
    wq_ref, own_ref, mine_ref, other_ref, kv_ref, tail_ref, stream, normed, weights = refs
    ctx = lax.axis_index("ctx")
    own, core = lax.rem(ctx, PLANE), lax.rem(ctx, 2)
    rows, wide = own_ref.shape[0], quarters[0].shape[1]
    fill_weights(ctx, weight_refs, weights)
    for i, ref in enumerate(quarters):
        start = ((core ^ (i // 2)) * 2 + i % 2) * wide
        stream[:, pl.ds(pl.multiple_of(start, wide), wide)] = ref[...]
    normed[...] = rms_rows(stream[...])
    own_ref[...] = stream[pl.ds(pl.multiple_of(own * rows, rows), rows), :]
    keyvals = dot(normed[...], weights[...]).astype(jnp.bfloat16)
    kv_ref[...] = keyvals
    tail_ref[...] = keyvals[keyvals.shape[0] - tail_ref.shape[0] :]
    project_query(normed[...], wq_ref, mine_ref, other_ref)


def mask_kernel(*refs):
    x_refs, (past_ref, bias_ref) = refs[:PLANE], refs[PLANE:]
    rows = bias_ref.shape[1]
    ctx = lax.axis_index("ctx")
    own = lax.rem(ctx, PLANE)
    before = WINDOW - 1
    columns = [group_ids(x_refs, own, g) for g in range(PLANE)]
    past = past_ref[before * rows :, :rows].astype(jnp.float32)
    keys = [jnp.broadcast_to(past[t : t + 1], (rows, rows)) for t in range(before)]
    keys += [jnp.transpose(column) for column in columns]
    causal = lax.broadcasted_iota(jnp.int32, (rows, rows), 0) >= lax.broadcasted_iota(
        jnp.int32, (rows, rows), 1
    )
    for g in range(PLANE):
        for t in range(WINDOW):
            allowed = columns[g] == keys[g + t]
            if t == before:
                allowed = allowed & causal
            if g + t < before:
                allowed = allowed & (ctx >= PLANE)
            bias_ref[g, :, t * rows : (t + 1) * rows] = jnp.where(allowed, 0.0, -jnp.inf)


def attend_kernel(layer, mine_ref, got_ref, bias_ref, kv_ref, past_ref, *refs):
    out_refs, window = refs[:-1], refs[-1]
    rows = bias_ref.shape[1]
    part = mine_ref.shape[1]
    tall, past = kv_ref.shape[0], (WINDOW - 1) * rows
    local_query = lax.rem(lax.axis_index("phase"), 2) == layer
    window[tall - past : tall] = past_ref[:past]
    window[tall:] = kv_ref[...]
    own = lax.rem(lax.axis_index("ctx"), PLANE)
    for g in range(PLANE):
        keys = window[(g + 1) * rows : (g + 1 + WINDOW) * rows]
        for h in range(0, part, HEAD):
            at = (slice(g * rows, (g + 1) * rows), slice(h, h + HEAD))
            query = jnp.where(local_query, mine_ref[at], got_ref[at])
            scores = lax.dot_general(
                query, keys[:, h : h + HEAD], (((1,), (1,)), ((), ())),
                preferred_element_type=jnp.float32,
            )
            scores = scores * (1.0 / math.sqrt(HEAD)) + bias_ref[g]
            weights = jnp.exp(scores - jnp.max(scores, axis=1, keepdims=True))
            total = jnp.sum(weights, axis=1, keepdims=True)
            values = keys[:, part + h : part + h + HEAD]
            result = (dot(weights.astype(jnp.bfloat16), values) / total).astype(jnp.bfloat16)
            if layer == 0:
                out_refs[0][g * rows : (g + 1) * rows, h : h + HEAD] = result
                continue
            place = pl.multiple_of(jnp.where(own // 2 == g // 2, 0, rows), rows)

            def put(ref):
                ref[pl.ds(place, rows), h : h + HEAD] = result

            pl.when(lax.rem(own, 2) == g % 2)(functools.partial(put, out_refs[0]))
            pl.when(lax.rem(own, 2) != g % 2)(functools.partial(put, out_refs[1]))


def pair_kernel(kept_ref, got_ref, mine_ref, other_ref):
    rows = kept_ref.shape[0] // 2
    for i, ref in enumerate((mine_ref, other_ref)):
        ref[:rows] = kept_ref[i * rows : (i + 1) * rows]
        ref[rows:] = got_ref[i * rows : (i + 1) * rows]


def last_kernel(*refs):
    b_refs, (wo_ref, own_ref, out_ref, blended) = refs[:PLANE], refs[PLANE:]
    own = lax.rem(lax.axis_index("ctx"), PLANE)
    side = lax.rem(lax.axis_index("phase"), 2)
    rows, part = own_ref.shape[0], b_refs[0].shape[1]

    @pl.when(side == 0)
    def _():
        out_ref[...] = own_ref[...]

    @pl.when(side == 1)
    def _():
        for m in range(2 * PLANE):
            place = pl.multiple_of(((side * PLANE + own) ^ m) * part, part)
            at = slice(m % 2 * rows, (m % 2 + 1) * rows)
            blended[:, pl.ds(place, part)] = b_refs[m // 2][at, :]
        total = own_ref[...].astype(jnp.float32) + dot(blended[...], wo_ref[...])
        out_ref[...] = total.astype(jnp.bfloat16)


def after(value, *others):
    return lax.optimization_barrier((value,) + others)[0]


def token_of(*blocks, cost):
    places = {i: pl.ANY for i in range(len(blocks))}
    return call(token_kernel, [((8, HEAD), jnp.float32)], [], cost, *blocks, far=places)[0]


def sooner(block):
    return after(block, token_of(block, cost=4 * 10**8))


def along_planes(piece, gate=()):
    held = {0: piece, 2: swap(after(piece, *gate), 0, PLANE * 2)}
    for m in range(4, lax.axis_size("ctx") // PLANE):
        held[m] = swap(after(piece, *gate), 0, PLANE * m)
    return held


def local(inputs, segment_ids, w_query, w_keyval, w_out):
    batches, rows, width = inputs.shape
    phases = lax.axis_size("phase")
    phase = lax.axis_index("phase")
    side = phase % 2
    own = lax.axis_index("ctx") % PLANE
    bf16 = jnp.bfloat16

    head_width = w_query.shape[2]
    part = head_width // (2 * PLANE)
    depth = w_keyval.shape[1]
    tall, past = PLANE * rows, (WINDOW - 1) * rows

    unit, half = head_width // 16, width // 2
    sent_first, sent_second, query_mat = call(
        slice_kernel,
        [((6 * unit, half), bf16), ((4 * unit, half), bf16), ((width, 2 * part), bf16)],
        [pltpu.SemaphoreType.DMA((5,))], LONG, w_out[0], w_query[0], far={0: pltpu.HBM, 1: pltpu.HBM},
    )

    kept, for_y, for_x, for_both = call(
        cut_kernel, [((depth, 4 * part), bf16)] * 4, [], 0, w_keyval[0]
    )
    across_both, across_x, across_y = swap(for_both, 1, 2), swap(for_x, 1, 0), swap(for_y, 0, 2)
    kept, sent_first, sent_second, query_mat = lax.optimization_barrier(
        (kept, sent_first, sent_second, query_mat)
    )
    near, far = call(
        sort_kernel, [((2, 2 * depth, 2 * part), bf16)] * 2, [], 0,
        kept, across_y, across_x, across_both,
    )
    piece = (4 * depth, 2 * part)
    early, late_start = call(
        merge_kernel, [(piece, bf16)] * 2, [], 0, near, swap(far, 0, 1)
    )
    out_first = swap(after(sent_first, across_y), 1, 0)
    shared = {}
    sent_on = call(copy_kernel, [((6 * unit, half), bf16)], [], 4 * 10**9, out_first)[0]
    out_across = swap(sent_on, 0, 2)
    early = along_planes(early)
    early[1] = swap(early[0], 0, PLANE)
    ready = token_of(token_of(early[2], cost=7 * 10**8), early[1], cost=24 * 10**8)
    early[3] = swap(after(early[2], ready), 0, PLANE)
    pieces = len(early)

    keyval_out = [((tall, 2 * part), bf16), ((past, 2 * part), bf16)]
    first_out = [((tall, 2 * part), bf16), ((past + 16, 2 * part), bf16)]
    query_out = [((tall, part), bf16)] * 2
    weights = ((width, 2 * part), bf16)
    dot_flops = 2 * tall * width * 2 * part
    attend_flops = 4 * tall * WINDOW * rows * part

    def two_layers(x, ids, bias):
        x = call(extend_kernel, [((rows, width + HEAD), bf16)], [], 0, x, ids)[0]
        across = swap(after(x, early[0]), 0, 2)
        xs = [x, across] + [swap(after(b, ready), 0, 1) for b in (x, across)]
        normed, mine, other, ids = call(
            query_kernel, [((tall, width), bf16)] + query_out + [((16, 2 * part), bf16)], [], 0,
            *xs, query_mat,
        )
        if not shared:
            shared["out"] = swap(after(sent_second, mine), 1, 0)
        kv, tail = call(
            functools.partial(keyval_kernel, pieces), first_out, [weights], LONG,
            *(early[m] for m in range(pieces)), normed, ids,
        )
        query = swap(other, 1, 0)
        late = along_planes(late_start, (kv,))
        late[1] = swap(after(late_start, kv), 0, PLANE)
        past_kv = from_plane_behind(tail)
        if bias is None:
            shape = ((PLANE, rows, WINDOW * rows), jnp.float32)
            bias = call(mask_kernel, [shape], [], 6 * 10**8, *xs, after(past_kv, query))[0]
        bias, *out = lax.optimization_barrier((bias, out_first, shared["out"], out_across))
        blended = call(
            functools.partial(attend_kernel, 0), [((tall, part), bf16)],
            [((2 * tall, 2 * part), bf16)], 0, mine, query, bias, kv, past_kv,
        )[0]
        near = [blended, swap(blended, 0, 2), swap(blended, 1, 0), sooner(swap(blended, 1, 2))]
        heads = [b for n in near for b in (n, swap(n, 0, 1))]
        late[3] = swap(after(late[2], late[1], near[2], near[3]), 0, PLANE)
        quarters = [
            call(
                functools.partial(stream_kernel, i), [((tall, width // 4), bf16)],
                [((tall, head_width), bf16), ((head_width, width // 4), bf16),
                 pltpu.SemaphoreType.DMA((4,))],
                0, *xs, *heads, w_out[0], *out,
                far={3 * PLANE + i: pltpu.HBM for i in range(4)},
            )[0]
            for i in range(2)
        ]
        quarters += [swap(quarters[0], 0, 1), swap(after(quarters[1], late[3]), 0, 1)]
        stream, mine, other, kv, tail = call(
            functools.partial(second_kernel, pieces),
            [((rows, width), bf16)] + query_out + keyval_out,
            [((tall, width), bf16), ((tall, width), bf16), weights], 0,
            *quarters, *(late[m] for m in range(pieces)), query_mat,
        )
        kept, given = call(
            functools.partial(attend_kernel, 1), [((tall // 2, part), bf16)] * 2,
            [((2 * tall, 2 * part), bf16)],
            attend_flops, mine, swap(other, 1, 0), bias, kv, from_plane_behind(tail),
        )
        mine, other = call(
            pair_kernel, [((tall // 2, part), bf16)] * 2, [], 0, kept, swap(given, 0, 1)
        )
        heads = [mine, swap(other, 0, 2), swap(mine, 1, 0), sooner(swap(other, 1, 2))]
        out = call(
            last_kernel, [((rows, width), bf16)], [((rows, head_width), bf16)],
            2 * rows * head_width * width, *heads, w_out[0], stream,
        )[0]
        return out, bias

    outs = []
    for b in range(batches):
        x, out, bias = inputs[b], None, None
        for tick in range(phases // 2):
            result, bias = two_layers(x, segment_ids[b : b + 1], bias)
            out = result if out is None else jnp.where(phase // 2 == tick, result, out)
            if tick + 1 < phases // 2:
                ahead = [
                    lax.ppermute(result, "phase", [(f, f + d) for f in range(1, phases - d, 2)])
                    for d in (1, 2)
                ]
                x = jnp.where(side == 0, ahead[0], ahead[1])
        outs.append(out)
    return jnp.stack(outs)[None]


def solution(mesh):
    placed = (
        P(None, "ctx", None),
        P(None, "ctx"),
        P("phase", None, None),
        P("phase", "ctx", None),
        P("phase", None, None),
    )
    return jax.shard_map(
        local, mesh=mesh, in_specs=placed, out_specs=P("phase", None, "ctx", None), check_vma=False
    )
```

```python
import functools
import math

import jax
import jax.numpy as jnp
from jax import lax
from jax.experimental import pallas as pl
from jax.experimental.pallas import tpu as pltpu
from jax.sharding import PartitionSpec as P

HEAD = 128
WINDOW = 4
PLANE = 4
FIRST, REST = 11, 5
ORDER = (0, 2, 1, 3)
BOTH = ("phase", "ctx")
VMEM_BYTES = 24 * 1024 * 1024
LONG = 10**11


def swap(block, phase_bit, ctx_bits):
    wide = lax.axis_size("ctx")
    route = [
        (f * wide + d, (f ^ phase_bit) * wide + (d ^ ctx_bits))
        for f in range(lax.axis_size("phase"))
        for d in range(wide)
    ]
    return lax.ppermute(block, BOTH, route)


def from_plane_behind(block):
    wide = lax.axis_size("ctx")
    return lax.ppermute(block, "ctx", [(i, i + PLANE) for i in range(wide - PLANE)])


def rms_rows(values):
    widened = values.astype(jnp.float32)
    scale = lax.rsqrt(jnp.mean(widened * widened, axis=-1, keepdims=True) + 1e-05)
    return (widened * scale).astype(jnp.bfloat16)


def dot(a, b):
    return jnp.dot(a, b, preferred_element_type=jnp.float32)


def call(kernel, outs, scratch, flops, *operands, far={}):
    moved = sum(o.size * o.dtype.itemsize for o in operands)
    place = lambda i: far.get(i, pltpu.VMEM)
    return pl.pallas_call(
        kernel,
        out_shape=[jax.ShapeDtypeStruct(s, d) for s, d in outs],
        in_specs=[pl.BlockSpec(memory_space=place(i)) for i in range(len(operands))],
        out_specs=[pl.BlockSpec(memory_space=pltpu.VMEM)] * len(outs),
        scratch_shapes=[pltpu.VMEM(*s) if isinstance(s, tuple) else s for s in scratch],
        cost_estimate=pl.CostEstimate(flops=flops, bytes_accessed=moved, transcendentals=0),
        compiler_params=pltpu.CompilerParams(vmem_limit_bytes=VMEM_BYTES),
    )(*operands)


def extend_kernel(x_ref, id_ref, out_ref):
    rows, width = x_ref.shape
    lanes = out_ref.shape[1] - width
    out_ref[:, :width] = x_ref[...]
    ids = jnp.broadcast_to(id_ref[...].astype(jnp.float32), (rows, rows))
    out_ref[:, width:] = jnp.broadcast_to(
        jnp.transpose(ids)[:, :1], (rows, lanes)
    ).astype(jnp.bfloat16)


def slice_kernel(out_ref, query_ref, sent_first, sent_second, query_mat, sems):
    side = lax.rem(lax.axis_index("phase"), 2)
    own = lax.rem(lax.axis_index("ctx"), PLANE)
    unit, wide = sent_first.shape[0] // FIRST, sent_first.shape[1]
    part = query_mat.shape[1] // 2
    columns = pl.ds(pl.multiple_of(lax.rem(own, 2) * wide, wide), wide)
    copies = []
    for i, (ref, first, count, upper, skip) in enumerate((
        (sent_first, 0, FIRST, own // 2, REST), (sent_second, 0, REST, own // 2, 0),
        (sent_second, REST, REST, 1 - own // 2, 0),
    )):
        at = pl.ds(pl.multiple_of((upper * (FIRST + REST) + skip) * unit, unit), count * unit)
        to = ref.at[pl.ds(first * unit, count * unit)]
        copies.append(pltpu.make_async_copy(out_ref.at[at, columns], to, sems.at[i]))
    for flip in (0, 1):
        at = pl.ds(pl.multiple_of(((side ^ flip) * PLANE + own) * part, part), part)
        to = query_mat.at[:, pl.ds(flip * part, part)]
        copies.append(pltpu.make_async_copy(query_ref.at[:, at], to, sems.at[3 + flip]))
    for copy in copies:
        copy.start()
    for copy in copies:
        copy.wait()


def cut_kernel(w_ref, *out_refs):
    side = lax.rem(lax.axis_index("phase"), 2)
    upper = lax.rem(lax.axis_index("ctx"), PLANE) // 2
    half = w_ref.shape[1] // 2
    pair = out_refs[0].shape[1] // 2
    for ref, (flip_side, flip_upper) in zip(out_refs, ((0, 0), (0, 1), (1, 0), (1, 1))):
        place = ((side ^ flip_side) * 2 + (upper ^ flip_upper)) * pair
        ref[:, :pair] = w_ref[:, pl.ds(pl.multiple_of(place, pair), pair)]
        ref[:, pair:] = w_ref[:, pl.ds(pl.multiple_of(place + half, pair), pair)]


def sort_kernel(kept, across_y, across_x, across_both, near_ref, far_ref):
    side = lax.rem(lax.axis_index("phase"), 2)
    core = lax.rem(lax.axis_index("ctx"), 2)
    rows, part = kept.shape[0], kept.shape[1] // 4
    for layer in range(2):
        for flip, out_ref in enumerate((near_ref, far_ref)):
            head = pl.multiple_of((core ^ flip) * part, part)

            def put(sources):
                for r, ref in enumerate(sources):
                    at = slice(r * rows, (r + 1) * rows)
                    out_ref[layer, at, :part] = ref[:, pl.ds(head, part)]
                    out_ref[layer, at, part:] = ref[:, pl.ds(head + 2 * part, part)]

            pl.when(side == layer)(functools.partial(put, (kept, across_y)))
            pl.when(side != layer)(functools.partial(put, (across_x, across_both)))


def merge_kernel(near_ref, far_ref, early_ref, late_ref):
    rows = near_ref.shape[1]
    for layer, ref in enumerate((early_ref, late_ref)):
        ref[:rows] = near_ref[layer]
        ref[rows:] = far_ref[layer]


def token_kernel(*refs):
    refs[-1][...] = jnp.zeros(refs[-1].shape, refs[-1].dtype)


def copy_kernel(block_ref, out_ref):
    out_ref[...] = block_ref[...]


def fill_weights(ctx, weight_refs, weights):
    rows = weight_refs[0].shape[0] // PLANE
    for m, ref in enumerate(weight_refs):
        for r, o in enumerate(ORDER):
            source = ctx ^ (PLANE * m + o)
            at = pl.ds(pl.multiple_of(source * rows, rows), rows)
            weights[at, :] = ref[r * rows : (r + 1) * rows, :]


def project_query(normed, wq_ref, mine_ref, other_ref):
    queries = dot(normed, wq_ref[...]).astype(jnp.bfloat16)
    part = mine_ref.shape[1]
    mine_ref[...] = queries[:, :part]
    other_ref[...] = queries[:, part:]


def norm_kernel(*refs):
    x_refs, (normed_ref,) = refs[:PLANE], refs[PLANE:]
    rows = x_refs[0].shape[0]
    own = lax.rem(lax.axis_index("ctx"), PLANE)
    for r, o in enumerate(ORDER):
        at = pl.ds(pl.multiple_of((own ^ o) * rows, rows), rows)
        normed_ref[at, :] = rms_rows(x_refs[r][:, : normed_ref.shape[1]])


def group_ids(x_refs, own, group):
    rows, width = x_refs[0].shape[0], x_refs[0].shape[1] - HEAD
    column = jnp.zeros((rows, 1), jnp.float32)
    for r, o in enumerate(ORDER):
        chosen = jnp.where((own ^ o) == group, 1.0, 0.0)
        column = column + chosen * x_refs[r][:, width : width + 1].astype(jnp.float32)
    return jnp.broadcast_to(column, (rows, rows))


def query_kernel(*refs):
    x_refs, (wq_ref, normed_ref, mine_ref, other_ref, ids_ref) = refs[:PLANE], refs[PLANE:]
    own, rows = lax.rem(lax.axis_index("ctx"), PLANE), x_refs[0].shape[0]
    norm_kernel(*x_refs, normed_ref)
    project_query(normed_ref[...], wq_ref, mine_ref, other_ref)
    extra, wide = ids_ref.shape
    line = lax.broadcasted_iota(jnp.int32, (extra, rows), 0)
    block = jnp.zeros((extra, rows), jnp.float32)
    for t in range(WINDOW - 1):
        row = jnp.transpose(group_ids(x_refs, own, PLANE - WINDOW + 1 + t))[:extra]
        block = jnp.where(line == t, row, block)
    ids_ref[:, :rows] = block.astype(jnp.bfloat16)
    ids_ref[:, rows:] = jnp.zeros((extra, wide - rows), jnp.bfloat16)


def keyval_kernel(pieces, *refs):
    weight_refs, (normed_ref, ids_ref, kv_ref, tail_ref, weights) = refs[:pieces], refs[pieces:]
    fill_weights(lax.axis_index("ctx"), weight_refs, weights)
    keyvals = dot(normed_ref[...], weights[...]).astype(jnp.bfloat16)
    kv_ref[...] = keyvals
    past = tail_ref.shape[0] - ids_ref.shape[0]
    tail_ref[:past] = keyvals[keyvals.shape[0] - past :]
    tail_ref[past:] = ids_ref[...]


def out_copies(own, first_column, local_ref, piece_refs, whole, sems):
    first_ref, second_ref, across_ref = piece_refs
    rows, wide = first_ref.shape[0] // FIRST, first_ref.shape[1]
    count_columns = whole.shape[1]
    start = lax.rem(own, 2) * wide + first_column
    columns = pl.ds(pl.multiple_of(start, count_columns), count_columns)
    piece_columns = pl.ds(first_column, count_columns)
    upper, half = own // 2, FIRST + REST
    from_own, from_pieces = [], []
    for i, (ref, first, place, count) in enumerate((
        (first_ref, 0, upper * half + REST, FIRST), (second_ref, 0, upper * half, REST),
        (second_ref, REST, (1 - upper) * half, REST),
        (across_ref, 0, (1 - upper) * half + REST, FIRST),
    )):
        at = pl.ds(pl.multiple_of(place * rows, rows), count * rows)
        source = ref.at[pl.ds(first * rows, count * rows), piece_columns]
        from_own.append(
            pltpu.make_async_copy(local_ref.at[at, columns], whole.at[at], sems.at[i])
        )
        from_pieces.append(pltpu.make_async_copy(source, whole.at[at], sems.at[i]))
    return from_own, from_pieces


def stream_kernel(part_index, *refs):
    x_refs, b_refs = refs[:PLANE], refs[PLANE : 3 * PLANE]
    wo_ref, piece_refs = refs[3 * PLANE], refs[3 * PLANE + 1 : 3 * PLANE + 4]
    half_ref, blended, whole, sems = refs[3 * PLANE + 4 :]
    side = lax.rem(lax.axis_index("phase"), 2)
    own = lax.rem(lax.axis_index("ctx"), PLANE)
    wide = half_ref.shape[1]
    from_own, from_pieces = out_copies(own, part_index * wide, wo_ref, piece_refs, whole, sems)

    @pl.when(side == 0)
    def _():
        for copy in from_own:
            copy.start()

    @pl.when(side == 1)
    def _():
        for copy in from_pieces:
            copy.start()

    rows, part = x_refs[0].shape[0], b_refs[0].shape[1]
    start = (lax.rem(own, 2) * 2 + part_index) * wide
    columns = pl.ds(pl.multiple_of(start, wide), wide)
    for r, o in enumerate(ORDER):
        at = pl.ds(pl.multiple_of((own ^ o) * rows, rows), rows)
        half_ref[at, :] = x_refs[r][:, columns]
    for m, ref in enumerate(b_refs):
        place = (side * PLANE + own) ^ m
        blended[:, pl.ds(pl.multiple_of(place * part, part), part)] = ref[...]
    for copy in from_own:
        copy.wait()
    step = min(512, wide)
    for n in range(0, wide, step):
        total = dot(blended[...], whole[:, n : n + step])
        total = total + half_ref[:, n : n + step].astype(jnp.float32)
        half_ref[:, n : n + step] = total.astype(jnp.bfloat16)


def second_kernel(pieces, *refs):
    quarters, refs = refs[:4], refs[4:]
    weight_refs, refs = refs[:pieces], refs[pieces:]
    wq_ref, own_ref, mine_ref, other_ref, kv_ref, tail_ref, stream, normed, weights = refs
    ctx = lax.axis_index("ctx")
    own, core = lax.rem(ctx, PLANE), lax.rem(ctx, 2)
    rows, wide = own_ref.shape[0], quarters[0].shape[1]
    fill_weights(ctx, weight_refs, weights)
    for i, ref in enumerate(quarters):
        start = ((core ^ (i // 2)) * 2 + i % 2) * wide
        stream[:, pl.ds(pl.multiple_of(start, wide), wide)] = ref[...]
    normed[...] = rms_rows(stream[...])
    own_ref[...] = stream[pl.ds(pl.multiple_of(own * rows, rows), rows), :]
    keyvals = dot(normed[...], weights[...]).astype(jnp.bfloat16)
    kv_ref[...] = keyvals
    tail_ref[...] = keyvals[keyvals.shape[0] - tail_ref.shape[0] :]
    project_query(normed[...], wq_ref, mine_ref, other_ref)


def mask_kernel(*refs):
    x_refs, (past_ref, bias_ref) = refs[:PLANE], refs[PLANE:]
    rows = bias_ref.shape[1]
    ctx = lax.axis_index("ctx")
    own = lax.rem(ctx, PLANE)
    before = WINDOW - 1
    columns = [group_ids(x_refs, own, g) for g in range(PLANE)]
    past = past_ref[before * rows :, :rows].astype(jnp.float32)
    keys = [jnp.broadcast_to(past[t : t + 1], (rows, rows)) for t in range(before)]
    keys += [jnp.transpose(column) for column in columns]
    causal = lax.broadcasted_iota(jnp.int32, (rows, rows), 0) >= lax.broadcasted_iota(
        jnp.int32, (rows, rows), 1
    )
    for g in range(PLANE):
        for t in range(WINDOW):
            allowed = columns[g] == keys[g + t]
            if t == before:
                allowed = allowed & causal
            if g + t < before:
                allowed = allowed & (ctx >= PLANE)
            bias_ref[g, :, t * rows : (t + 1) * rows] = jnp.where(allowed, 0.0, -jnp.inf)


def attend_kernel(layer, mine_ref, got_ref, bias_ref, kv_ref, past_ref, *refs):
    if layer == 0:
        whole, window = refs
    else:
        out_refs, whole, window = refs[:2], refs[2], refs[3]
    rows = bias_ref.shape[1]
    part = mine_ref.shape[1]
    tall, past = kv_ref.shape[0], (WINDOW - 1) * rows
    local_query = lax.rem(lax.axis_index("phase"), 2) == layer
    window[tall - past : tall] = past_ref[:past]
    window[tall:] = kv_ref[...]
    own = lax.rem(lax.axis_index("ctx"), PLANE)
    for g in range(PLANE):
        keys = window[(g + 1) * rows : (g + 1 + WINDOW) * rows]
        for h in range(0, part, HEAD):
            at = (slice(g * rows, (g + 1) * rows), slice(h, h + HEAD))
            query = jnp.where(local_query, mine_ref[at], got_ref[at])
            scores = lax.dot_general(
                query, keys[:, h : h + HEAD], (((1,), (1,)), ((), ())),
                preferred_element_type=jnp.float32,
            )
            scores = scores * (1.0 / math.sqrt(HEAD)) + bias_ref[g]
            weights = jnp.exp(scores - jnp.max(scores, axis=1, keepdims=True))
            total = jnp.sum(weights, axis=1, keepdims=True)
            values = keys[:, part + h : part + h + HEAD]
            result = (dot(weights.astype(jnp.bfloat16), values) / total).astype(jnp.bfloat16)
            whole[g * rows : (g + 1) * rows, h : h + HEAD] = result
    if layer == 0:
        return
    for core, ref in enumerate(out_refs):
        for i in range(2):
            group = 2 * (own // 2 ^ i) + (own % 2 ^ core)
            place = pl.multiple_of(group * rows, rows)
            ref[i * rows : (i + 1) * rows, :] = whole[pl.ds(place, rows), :]


def pair_kernel(kept_ref, got_ref, mine_ref, other_ref):
    rows = kept_ref.shape[0] // 2
    for i, ref in enumerate((mine_ref, other_ref)):
        ref[:rows] = kept_ref[i * rows : (i + 1) * rows]
        ref[rows:] = got_ref[i * rows : (i + 1) * rows]


def last_kernel(*refs):
    b_refs, (wo_ref, own_ref, out_ref, blended) = refs[:PLANE], refs[PLANE:]
    own = lax.rem(lax.axis_index("ctx"), PLANE)
    side = lax.rem(lax.axis_index("phase"), 2)
    rows, part = own_ref.shape[0], b_refs[0].shape[1]

    @pl.when(side == 0)
    def _():
        out_ref[...] = own_ref[...]

    @pl.when(side == 1)
    def _():
        for m in range(2 * PLANE):
            place = pl.multiple_of(((side * PLANE + own) ^ m) * part, part)
            at = slice(m % 2 * rows, (m % 2 + 1) * rows)
            blended[:, pl.ds(place, part)] = b_refs[m // 2][at, :]
        total = own_ref[...].astype(jnp.float32) + dot(blended[...], wo_ref[...])
        out_ref[...] = total.astype(jnp.bfloat16)


def after(value, *others):
    return lax.optimization_barrier((value,) + others)[0]


def token_of(*blocks, cost):
    places = {i: pl.ANY for i in range(len(blocks))}
    return call(token_kernel, [((8, HEAD), jnp.float32)], [], cost, *blocks, far=places)[0]


def sooner(block, cost=4 * 10**8):
    return after(block, token_of(block, cost=cost))


def along_planes(piece, gate=()):
    held = {0: piece, 2: swap(after(piece, *gate), 0, PLANE * 2)}
    for m in range(4, lax.axis_size("ctx") // PLANE):
        held[m] = swap(after(piece, *gate), 0, PLANE * m)
    return held


def local(inputs, segment_ids, w_query, w_keyval, w_out):
    batches, rows, width = inputs.shape
    phases = lax.axis_size("phase")
    phase = lax.axis_index("phase")
    side = phase % 2
    own = lax.axis_index("ctx") % PLANE
    bf16 = jnp.bfloat16

    head_width = w_query.shape[2]
    part = head_width // (2 * PLANE)
    depth = w_keyval.shape[1]
    tall, past = PLANE * rows, (WINDOW - 1) * rows

    unit, half = head_width // (2 * (FIRST + REST)), width // 2
    sent_first, sent_second, query_mat = call(
        slice_kernel,
        [((FIRST * unit, half), bf16), ((2 * REST * unit, half), bf16), ((width, 2 * part), bf16)],
        [pltpu.SemaphoreType.DMA((5,))], LONG, w_out[0], w_query[0], far={0: pltpu.HBM, 1: pltpu.HBM},
    )

    kept, for_y, for_x, for_both = call(
        cut_kernel, [((depth, 4 * part), bf16)] * 4, [], 0, w_keyval[0]
    )
    across_both, across_x, across_y = swap(for_both, 1, 2), swap(for_x, 1, 0), swap(for_y, 0, 2)
    kept, sent_first, sent_second, query_mat = lax.optimization_barrier(
        (kept, sent_first, sent_second, query_mat)
    )
    near, far = call(
        sort_kernel, [((2, 2 * depth, 2 * part), bf16)] * 2, [], 0,
        kept, across_y, across_x, across_both,
    )
    piece = (4 * depth, 2 * part)
    early, late_start = call(
        merge_kernel, [(piece, bf16)] * 2, [], 0, near, swap(far, 0, 1)
    )
    out_first = swap(after(sent_first, across_y), 1, 0)
    shared = {}
    sent_on = call(copy_kernel, [((FIRST * unit, half), bf16)], [], 6 * 10**9, out_first)[0]
    out_across = swap(sent_on, 0, 2)
    early = along_planes(early)
    early[1] = swap(early[0], 0, PLANE)
    ready = token_of(token_of(early[2], cost=7 * 10**8), early[1], cost=24 * 10**8)
    early[3] = swap(after(early[2], ready), 0, PLANE)
    pieces = len(early)

    keyval_out = [((tall, 2 * part), bf16), ((past, 2 * part), bf16)]
    first_out = [((tall, 2 * part), bf16), ((past + 16, 2 * part), bf16)]
    query_out = [((tall, part), bf16)] * 2
    weights = ((width, 2 * part), bf16)
    dot_flops = 2 * tall * width * 2 * part
    attend_flops = 4 * tall * WINDOW * rows * part

    def two_layers(x, ids, bias):
        x = call(extend_kernel, [((rows, width + HEAD), bf16)], [], 0, x, ids)[0]
        across = swap(after(x, early[0]), 0, 2)
        xs = [x, across] + [swap(after(b, ready), 0, 1) for b in (x, across)]
        normed, mine, other, ids = call(
            query_kernel, [((tall, width), bf16)] + query_out + [((16, 2 * part), bf16)], [], 0,
            *xs, query_mat,
        )
        if not shared:
            shared["out"] = swap(after(sent_second, mine), 1, 0)
        kv, tail = call(
            functools.partial(keyval_kernel, pieces), first_out, [weights], LONG,
            *(early[m] for m in range(pieces)), normed, ids,
        )
        query = swap(other, 1, 0)
        late = along_planes(late_start, (kv,))
        late[1] = swap(after(late_start, kv), 0, PLANE)
        past_kv = from_plane_behind(tail)
        if bias is None:
            shape = ((PLANE, rows, WINDOW * rows), jnp.float32)
            bias = call(mask_kernel, [shape], [], 6 * 10**8, *xs, after(past_kv, query))[0]
        bias, first, across_out = lax.optimization_barrier((bias, out_first, out_across))
        blended = call(
            functools.partial(attend_kernel, 0), [((tall, part), bf16)],
            [((2 * tall, 2 * part), bf16)], 0, mine, query, bias, kv, past_kv,
        )[0]
        y_block, second = lax.optimization_barrier((blended, shared["out"]))
        out = [first, second, across_out]
        near = [blended, swap(y_block, 0, 2), swap(blended, 1, 0), sooner(swap(blended, 1, 2))]
        heads = [b for n in near for b in (n, swap(n, 0, 1))]
        late[3] = swap(after(late[2], late[1], near[3]), 0, PLANE)
        quarters = [
            call(
                functools.partial(stream_kernel, i), [((tall, width // 4), bf16)],
                [((tall, head_width), bf16), ((head_width, width // 4), bf16),
                 pltpu.SemaphoreType.DMA((4,))],
                0, *xs, *heads, w_out[0], *out,
                far={3 * PLANE + i: pltpu.HBM for i in range(4)},
            )[0]
            for i in range(2)
        ]
        quarters += [swap(quarters[0], 0, 1), swap(after(quarters[1], late[3]), 0, 1)]
        stream, mine, other, kv, tail = call(
            functools.partial(second_kernel, pieces),
            [((rows, width), bf16)] + query_out + keyval_out,
            [((tall, width), bf16), ((tall, width), bf16), weights], 0,
            *quarters, *(late[m] for m in range(pieces)), query_mat,
        )
        kept, given = call(
            functools.partial(attend_kernel, 1), [((tall // 2, part), bf16)] * 2,
            [((tall, part), bf16), ((2 * tall, 2 * part), bf16)],
            attend_flops, mine, swap(other, 1, 0), bias, kv, from_plane_behind(tail),
        )
        mine, other = call(
            pair_kernel, [((tall // 2, part), bf16)] * 2, [], 0, kept, swap(given, 0, 1)
        )
        heads = [mine, swap(other, 0, 2), swap(mine, 1, 0), sooner(swap(other, 1, 2))]
        out = call(
            last_kernel, [((rows, width), bf16)], [((rows, head_width), bf16)],
            2 * rows * head_width * width, *heads, w_out[0], stream,
        )[0]
        return out, bias

    outs = []
    for b in range(batches):
        x, out, bias = inputs[b], None, None
        for tick in range(phases // 2):
            result, bias = two_layers(x, segment_ids[b : b + 1], bias)
            out = result if out is None else jnp.where(phase // 2 == tick, result, out)
            if tick + 1 < phases // 2:
                ahead = [
                    lax.ppermute(result, "phase", [(f, f + d) for f in range(1, phases - d, 2)])
                    for d in (1, 2)
                ]
                x = jnp.where(side == 0, ahead[0], ahead[1])
        outs.append(out)
    return jnp.stack(outs)[None]


def solution(mesh):
    placed = (
        P(None, "ctx", None),
        P(None, "ctx"),
        P("phase", None, None),
        P("phase", "ctx", None),
        P("phase", None, None),
    )
    return jax.shard_map(
        local, mesh=mesh, in_specs=placed, out_specs=P("phase", None, "ctx", None), check_vma=False
    )
```

```python
import functools
import math

import jax
import jax.numpy as jnp
from jax import lax
from jax.experimental import pallas as pl
from jax.experimental.pallas import tpu as pltpu
from jax.sharding import PartitionSpec as P

HEAD = 128
WINDOW = 4
PLANE = 4
FIRST, REST = 11, 5
ORDER = (0, 2, 1, 3)
BOTH = ("phase", "ctx")
VMEM_BYTES = 24 * 1024 * 1024
LONG = 10**11


def swap(block, phase_bit, ctx_bits):
    wide = lax.axis_size("ctx")
    route = [
        (f * wide + d, (f ^ phase_bit) * wide + (d ^ ctx_bits))
        for f in range(lax.axis_size("phase"))
        for d in range(wide)
    ]
    return lax.ppermute(block, BOTH, route)


def from_plane_behind(block):
    wide = lax.axis_size("ctx")
    return lax.ppermute(block, "ctx", [(i, i + PLANE) for i in range(wide - PLANE)])


def rms_rows(values):
    widened = values.astype(jnp.float32)
    scale = lax.rsqrt(jnp.mean(widened * widened, axis=-1, keepdims=True) + 1e-05)
    return (widened * scale).astype(jnp.bfloat16)


def dot(a, b):
    return jnp.dot(a, b, preferred_element_type=jnp.float32)


def call(kernel, outs, scratch, flops, *operands, far={}):
    moved = sum(o.size * o.dtype.itemsize for o in operands)
    place = lambda i: far.get(i, pltpu.VMEM)
    return pl.pallas_call(
        kernel,
        out_shape=[jax.ShapeDtypeStruct(s, d) for s, d in outs],
        in_specs=[pl.BlockSpec(memory_space=place(i)) for i in range(len(operands))],
        out_specs=[pl.BlockSpec(memory_space=pltpu.VMEM)] * len(outs),
        scratch_shapes=[pltpu.VMEM(*s) if isinstance(s, tuple) else s for s in scratch],
        cost_estimate=pl.CostEstimate(flops=flops, bytes_accessed=moved, transcendentals=0),
        compiler_params=pltpu.CompilerParams(vmem_limit_bytes=VMEM_BYTES),
    )(*operands)


def extend_kernel(x_ref, id_ref, out_ref):
    rows, width = x_ref.shape
    lanes = out_ref.shape[1] - width
    out_ref[:, :width] = x_ref[...]
    ids = jnp.broadcast_to(id_ref[...].astype(jnp.float32), (rows, rows))
    out_ref[:, width:] = jnp.broadcast_to(
        jnp.transpose(ids)[:, :1], (rows, lanes)
    ).astype(jnp.bfloat16)


def slice_kernel(out_ref, query_ref, sent_first, sent_second, query_mat, sems):
    side = lax.rem(lax.axis_index("phase"), 2)
    own = lax.rem(lax.axis_index("ctx"), PLANE)
    unit, wide = sent_first.shape[0] // FIRST, sent_first.shape[1]
    part = query_mat.shape[1] // 2
    columns = pl.ds(pl.multiple_of(lax.rem(own, 2) * wide, wide), wide)
    copies = []
    for i, (ref, first, count, upper, skip) in enumerate((
        (sent_first, 0, FIRST, own // 2, REST), (sent_second, 0, REST, own // 2, 0),
        (sent_second, REST, REST, 1 - own // 2, 0),
    )):
        at = pl.ds(pl.multiple_of((upper * (FIRST + REST) + skip) * unit, unit), count * unit)
        to = ref.at[pl.ds(first * unit, count * unit)]
        copies.append(pltpu.make_async_copy(out_ref.at[at, columns], to, sems.at[i]))
    for flip in (0, 1):
        at = pl.ds(pl.multiple_of(((side ^ flip) * PLANE + own) * part, part), part)
        to = query_mat.at[:, pl.ds(flip * part, part)]
        copies.append(pltpu.make_async_copy(query_ref.at[:, at], to, sems.at[3 + flip]))
    for copy in copies:
        copy.start()
    for copy in copies:
        copy.wait()


def cut_kernel(w_ref, *out_refs):
    side = lax.rem(lax.axis_index("phase"), 2)
    upper = lax.rem(lax.axis_index("ctx"), PLANE) // 2
    half = w_ref.shape[1] // 2
    pair = out_refs[0].shape[1] // 2
    for ref, (flip_side, flip_upper) in zip(out_refs, ((0, 0), (0, 1), (1, 0), (1, 1))):
        place = ((side ^ flip_side) * 2 + (upper ^ flip_upper)) * pair
        ref[:, :pair] = w_ref[:, pl.ds(pl.multiple_of(place, pair), pair)]
        ref[:, pair:] = w_ref[:, pl.ds(pl.multiple_of(place + half, pair), pair)]


def sort_kernel(kept, across_y, across_x, across_both, near_ref, far_ref):
    side = lax.rem(lax.axis_index("phase"), 2)
    core = lax.rem(lax.axis_index("ctx"), 2)
    rows, part = kept.shape[0], kept.shape[1] // 4
    for layer in range(2):
        for flip, out_ref in enumerate((near_ref, far_ref)):
            head = pl.multiple_of((core ^ flip) * part, part)

            def put(sources):
                for r, ref in enumerate(sources):
                    at = slice(r * rows, (r + 1) * rows)
                    out_ref[layer, at, :part] = ref[:, pl.ds(head, part)]
                    out_ref[layer, at, part:] = ref[:, pl.ds(head + 2 * part, part)]

            pl.when(side == layer)(functools.partial(put, (kept, across_y)))
            pl.when(side != layer)(functools.partial(put, (across_x, across_both)))


def merge_kernel(near_ref, far_ref, early_ref, late_ref):
    rows = near_ref.shape[1]
    for layer, ref in enumerate((early_ref, late_ref)):
        ref[:rows] = near_ref[layer]
        ref[rows:] = far_ref[layer]


def token_kernel(*refs):
    refs[-1][...] = jnp.zeros(refs[-1].shape, refs[-1].dtype)


def copy_kernel(block_ref, out_ref):
    out_ref[...] = block_ref[...]


def fill_weights(ctx, weight_refs, weights):
    rows = weight_refs[0].shape[0] // PLANE
    for m, ref in enumerate(weight_refs):
        for r, o in enumerate(ORDER):
            source = ctx ^ (PLANE * m + o)
            at = pl.ds(pl.multiple_of(source * rows, rows), rows)
            weights[at, :] = ref[r * rows : (r + 1) * rows, :]


def project_query(normed, wq_ref, mine_ref, other_ref):
    queries = dot(normed, wq_ref[...]).astype(jnp.bfloat16)
    part = mine_ref.shape[1]
    mine_ref[...] = queries[:, :part]
    other_ref[...] = queries[:, part:]


def norm_kernel(*refs):
    x_refs, (normed_ref,) = refs[:PLANE], refs[PLANE:]
    rows = x_refs[0].shape[0]
    own = lax.rem(lax.axis_index("ctx"), PLANE)
    for r, o in enumerate(ORDER):
        at = pl.ds(pl.multiple_of((own ^ o) * rows, rows), rows)
        normed_ref[at, :] = rms_rows(x_refs[r][:, : normed_ref.shape[1]])


def group_ids(x_refs, own, group):
    rows, width = x_refs[0].shape[0], x_refs[0].shape[1] - HEAD
    column = jnp.zeros((rows, 1), jnp.float32)
    for r, o in enumerate(ORDER):
        chosen = jnp.where((own ^ o) == group, 1.0, 0.0)
        column = column + chosen * x_refs[r][:, width : width + 1].astype(jnp.float32)
    return jnp.broadcast_to(column, (rows, rows))


def query_kernel(*refs):
    x_refs, (wq_ref, normed_ref, mine_ref, other_ref, ids_ref) = refs[:PLANE], refs[PLANE:]
    own, rows = lax.rem(lax.axis_index("ctx"), PLANE), x_refs[0].shape[0]
    norm_kernel(*x_refs, normed_ref)
    project_query(normed_ref[...], wq_ref, mine_ref, other_ref)
    extra, wide = ids_ref.shape
    line = lax.broadcasted_iota(jnp.int32, (extra, rows), 0)
    block = jnp.zeros((extra, rows), jnp.float32)
    for t in range(WINDOW - 1):
        row = jnp.transpose(group_ids(x_refs, own, PLANE - WINDOW + 1 + t))[:extra]
        block = jnp.where(line == t, row, block)
    ids_ref[:, :rows] = block.astype(jnp.bfloat16)
    ids_ref[:, rows:] = jnp.zeros((extra, wide - rows), jnp.bfloat16)


def keyval_kernel(pieces, *refs):
    weight_refs, (normed_ref, ids_ref, kv_ref, tail_ref, weights) = refs[:pieces], refs[pieces:]
    fill_weights(lax.axis_index("ctx"), weight_refs, weights)
    keyvals = dot(normed_ref[...], weights[...]).astype(jnp.bfloat16)
    kv_ref[...] = keyvals
    past = tail_ref.shape[0] - ids_ref.shape[0]
    tail_ref[:past] = keyvals[keyvals.shape[0] - past :]
    tail_ref[past:] = ids_ref[...]


def out_copies(own, first_column, local_ref, piece_refs, whole, sems):
    first_ref, second_ref, across_ref = piece_refs
    rows, wide = first_ref.shape[0] // FIRST, first_ref.shape[1]
    count_columns = whole.shape[1]
    start = lax.rem(own, 2) * wide + first_column
    columns = pl.ds(pl.multiple_of(start, count_columns), count_columns)
    piece_columns = pl.ds(first_column, count_columns)
    upper, half = own // 2, FIRST + REST
    from_own, from_pieces = [], []
    for i, (ref, first, place, count) in enumerate((
        (first_ref, 0, upper * half + REST, FIRST), (second_ref, 0, upper * half, REST),
        (second_ref, REST, (1 - upper) * half, REST),
        (across_ref, 0, (1 - upper) * half + REST, FIRST),
    )):
        at = pl.ds(pl.multiple_of(place * rows, rows), count * rows)
        source = ref.at[pl.ds(first * rows, count * rows), piece_columns]
        from_own.append(
            pltpu.make_async_copy(local_ref.at[at, columns], whole.at[at], sems.at[i])
        )
        from_pieces.append(pltpu.make_async_copy(source, whole.at[at], sems.at[i]))
    return from_own, from_pieces


def stream_kernel(part_index, *refs):
    x_refs, b_refs = refs[:PLANE], refs[PLANE : 3 * PLANE]
    wo_ref, piece_refs = refs[3 * PLANE], refs[3 * PLANE + 1 : 3 * PLANE + 4]
    half_ref, blended, whole, sems = refs[3 * PLANE + 4 :]
    side = lax.rem(lax.axis_index("phase"), 2)
    own = lax.rem(lax.axis_index("ctx"), PLANE)
    wide = half_ref.shape[1]
    from_own, from_pieces = out_copies(own, part_index * wide, wo_ref, piece_refs, whole, sems)

    @pl.when(side == 0)
    def _():
        for copy in from_own:
            copy.start()

    @pl.when(side == 1)
    def _():
        for copy in from_pieces:
            copy.start()

    rows, part = x_refs[0].shape[0], b_refs[0].shape[1]
    start = (lax.rem(own, 2) * 2 + part_index) * wide
    columns = pl.ds(pl.multiple_of(start, wide), wide)
    for r, o in enumerate(ORDER):
        at = pl.ds(pl.multiple_of((own ^ o) * rows, rows), rows)
        half_ref[at, :] = x_refs[r][:, columns]
    for m, ref in enumerate(b_refs):
        place = (side * PLANE + own) ^ m
        blended[:, pl.ds(pl.multiple_of(place * part, part), part)] = ref[...]
    for copy in from_own:
        copy.wait()
    step = min(512, wide)
    for n in range(0, wide, step):
        total = dot(blended[...], whole[:, n : n + step])
        total = total + half_ref[:, n : n + step].astype(jnp.float32)
        half_ref[:, n : n + step] = total.astype(jnp.bfloat16)


def second_kernel(pieces, *refs):
    quarters, refs = refs[:4], refs[4:]
    weight_refs, refs = refs[:pieces], refs[pieces:]
    wq_ref, own_ref, mine_ref, other_ref, kv_ref, tail_ref, stream, normed, weights = refs
    ctx = lax.axis_index("ctx")
    own, core = lax.rem(ctx, PLANE), lax.rem(ctx, 2)
    rows, wide = own_ref.shape[0], quarters[0].shape[1]
    fill_weights(ctx, weight_refs, weights)
    for i, ref in enumerate(quarters):
        start = ((core ^ (i // 2)) * 2 + i % 2) * wide
        stream[:, pl.ds(pl.multiple_of(start, wide), wide)] = ref[...]
    normed[...] = rms_rows(stream[...])
    own_ref[...] = stream[pl.ds(pl.multiple_of(own * rows, rows), rows), :]
    keyvals = dot(normed[...], weights[...]).astype(jnp.bfloat16)
    kv_ref[...] = keyvals
    tail_ref[...] = keyvals[keyvals.shape[0] - tail_ref.shape[0] :]
    project_query(normed[...], wq_ref, mine_ref, other_ref)


def mask_kernel(*refs):
    x_refs, (past_ref, bias_ref) = refs[:PLANE], refs[PLANE:]
    rows = bias_ref.shape[1]
    ctx = lax.axis_index("ctx")
    own = lax.rem(ctx, PLANE)
    before = WINDOW - 1
    columns = [group_ids(x_refs, own, g) for g in range(PLANE)]
    past = past_ref[before * rows :, :rows].astype(jnp.float32)
    keys = [jnp.broadcast_to(past[t : t + 1], (rows, rows)) for t in range(before)]
    keys += [jnp.transpose(column) for column in columns]
    causal = lax.broadcasted_iota(jnp.int32, (rows, rows), 0) >= lax.broadcasted_iota(
        jnp.int32, (rows, rows), 1
    )
    for g in range(PLANE):
        for t in range(WINDOW):
            allowed = columns[g] == keys[g + t]
            if t == before:
                allowed = allowed & causal
            if g + t < before:
                allowed = allowed & (ctx >= PLANE)
            bias_ref[g, :, t * rows : (t + 1) * rows] = jnp.where(allowed, 0.0, -jnp.inf)


def attend_kernel(layer, mine_ref, got_ref, bias_ref, kv_ref, past_ref, *refs):
    if layer == 0:
        whole, window = refs
    else:
        out_refs, whole, window = refs[:2], refs[2], refs[3]
    rows = bias_ref.shape[1]
    part = mine_ref.shape[1]
    tall, past = kv_ref.shape[0], (WINDOW - 1) * rows
    local_query = lax.rem(lax.axis_index("phase"), 2) == layer
    window[tall - past : tall] = past_ref[:past]
    window[tall:] = kv_ref[...]
    own = lax.rem(lax.axis_index("ctx"), PLANE)
    for g in range(PLANE):
        keys = window[(g + 1) * rows : (g + 1 + WINDOW) * rows]
        for h in range(0, part, HEAD):
            at = (slice(g * rows, (g + 1) * rows), slice(h, h + HEAD))
            query = jnp.where(local_query, mine_ref[at], got_ref[at])
            scores = lax.dot_general(
                query, keys[:, h : h + HEAD], (((1,), (1,)), ((), ())),
                preferred_element_type=jnp.float32,
            )
            scores = scores * (1.0 / math.sqrt(HEAD)) + bias_ref[g]
            weights = jnp.exp(scores - jnp.max(scores, axis=1, keepdims=True))
            total = jnp.sum(weights, axis=1, keepdims=True)
            values = keys[:, part + h : part + h + HEAD]
            result = (dot(weights.astype(jnp.bfloat16), values) / total).astype(jnp.bfloat16)
            whole[g * rows : (g + 1) * rows, h : h + HEAD] = result
    if layer == 0:
        return
    for core, ref in enumerate(out_refs):
        for i in range(2):
            group = 2 * (own // 2 ^ i) + (own % 2 ^ core)
            place = pl.multiple_of(group * rows, rows)
            ref[i * rows : (i + 1) * rows, :] = whole[pl.ds(place, rows), :]


def pair_kernel(kept_ref, got_ref, mine_ref, other_ref):
    rows = kept_ref.shape[0] // 2
    for i, ref in enumerate((mine_ref, other_ref)):
        ref[:rows] = kept_ref[i * rows : (i + 1) * rows]
        ref[rows:] = got_ref[i * rows : (i + 1) * rows]


def last_kernel(*refs):
    b_refs, (wo_ref, own_ref, out_ref, blended) = refs[:PLANE], refs[PLANE:]
    own = lax.rem(lax.axis_index("ctx"), PLANE)
    side = lax.rem(lax.axis_index("phase"), 2)
    rows, part = own_ref.shape[0], b_refs[0].shape[1]

    @pl.when(side == 0)
    def _():
        out_ref[...] = own_ref[...]

    @pl.when(side == 1)
    def _():
        for m in range(2 * PLANE):
            place = pl.multiple_of(((side * PLANE + own) ^ m) * part, part)
            at = slice(m % 2 * rows, (m % 2 + 1) * rows)
            blended[:, pl.ds(place, part)] = b_refs[m // 2][at, :]
        total = own_ref[...].astype(jnp.float32) + dot(blended[...], wo_ref[...])
        out_ref[...] = total.astype(jnp.bfloat16)


def after(value, *others):
    return lax.optimization_barrier((value,) + others)[0]


def token_of(*blocks, cost):
    places = {i: pl.ANY for i in range(len(blocks))}
    return call(token_kernel, [((8, HEAD), jnp.float32)], [], cost, *blocks, far=places)[0]


def sooner(block, cost=4 * 10**8):
    return after(block, token_of(block, cost=cost))


def along_planes(piece, gate=()):
    held = {0: piece, 2: swap(after(piece, *gate), 0, PLANE * 2)}
    for m in range(4, lax.axis_size("ctx") // PLANE):
        held[m] = swap(after(piece, *gate), 0, PLANE * m)
    return held


def local(inputs, segment_ids, w_query, w_keyval, w_out):
    batches, rows, width = inputs.shape
    phases = lax.axis_size("phase")
    phase = lax.axis_index("phase")
    side = phase % 2
    own = lax.axis_index("ctx") % PLANE
    bf16 = jnp.bfloat16

    head_width = w_query.shape[2]
    part = head_width // (2 * PLANE)
    depth = w_keyval.shape[1]
    tall, past = PLANE * rows, (WINDOW - 1) * rows

    unit, half = head_width // (2 * (FIRST + REST)), width // 2
    sent_first, sent_second, query_mat = call(
        slice_kernel,
        [((FIRST * unit, half), bf16), ((2 * REST * unit, half), bf16), ((width, 2 * part), bf16)],
        [pltpu.SemaphoreType.DMA((5,))], LONG, w_out[0], w_query[0], far={0: pltpu.HBM, 1: pltpu.HBM},
    )

    kept, for_y, for_x, for_both = call(
        cut_kernel, [((depth, 4 * part), bf16)] * 4, [], 0, w_keyval[0]
    )
    across_both, across_x, across_y = swap(for_both, 1, 2), swap(for_x, 1, 0), swap(for_y, 0, 2)
    kept, sent_first, sent_second, query_mat = lax.optimization_barrier(
        (kept, sent_first, sent_second, query_mat)
    )
    near, far = call(
        sort_kernel, [((2, 2 * depth, 2 * part), bf16)] * 2, [], 0,
        kept, across_y, across_x, across_both,
    )
    piece = (4 * depth, 2 * part)
    early, late_start = call(
        merge_kernel, [(piece, bf16)] * 2, [], 0, near, swap(far, 0, 1)
    )
    out_first = swap(after(sent_first, across_y), 1, 0)
    shared = {}
    sent_on = call(copy_kernel, [((FIRST * unit, half), bf16)], [], 6 * 10**9, out_first)[0]
    out_across = swap(sent_on, 0, 2)
    early = along_planes(early)
    early[1] = swap(early[0], 0, PLANE)
    ready = token_of(token_of(early[2], cost=4 * 10**8), early[1], cost=35 * 10**8)
    early[3] = swap(after(early[2], ready), 0, PLANE)
    pieces = len(early)

    keyval_out = [((tall, 2 * part), bf16), ((past, 2 * part), bf16)]
    first_out = [((tall, 2 * part), bf16), ((past + 16, 2 * part), bf16)]
    query_out = [((tall, part), bf16)] * 2
    weights = ((width, 2 * part), bf16)
    dot_flops = 2 * tall * width * 2 * part
    attend_flops = 4 * tall * WINDOW * rows * part

    def two_layers(x, ids, bias):
        x = call(extend_kernel, [((rows, width + HEAD), bf16)], [], 0, x, ids)[0]
        across = swap(after(x, early[0]), 0, 2)
        xs = [x, across] + [swap(after(b, ready), 0, 1) for b in (x, across)]
        normed, mine, other, ids = call(
            query_kernel, [((tall, width), bf16)] + query_out + [((16, 2 * part), bf16)], [], 0,
            *xs, query_mat,
        )
        if not shared:
            shared["out"] = swap(after(sent_second, mine), 1, 0)
        kv, tail = call(
            functools.partial(keyval_kernel, pieces), first_out, [weights], LONG,
            *(early[m] for m in range(pieces)), normed, ids,
        )
        query = swap(other, 1, 0)
        late = along_planes(late_start, (kv,))
        late[1] = swap(after(late_start, kv), 0, PLANE)
        past_kv = from_plane_behind(tail)
        if bias is None:
            shape = ((PLANE, rows, WINDOW * rows), jnp.float32)
            bias = call(mask_kernel, [shape], [], 6 * 10**8, *xs, after(past_kv, query))[0]
        bias, first, across_out = lax.optimization_barrier((bias, out_first, out_across))
        blended = call(
            functools.partial(attend_kernel, 0), [((tall, part), bf16)],
            [((2 * tall, 2 * part), bf16)], 0, mine, query, bias, kv, past_kv,
        )[0]
        y_block, second = lax.optimization_barrier((blended, shared["out"]))
        out = [first, second, across_out]
        near = [blended, swap(y_block, 0, 2), swap(blended, 1, 0), sooner(swap(blended, 1, 2))]
        heads = [b for n in near for b in (n, swap(n, 0, 1))]
        late[3] = swap(after(late[2], late[1], near[3]), 0, PLANE)
        quarters = [
            call(
                functools.partial(stream_kernel, i), [((tall, width // 4), bf16)],
                [((tall, head_width), bf16), ((head_width, width // 4), bf16),
                 pltpu.SemaphoreType.DMA((4,))],
                0, *xs, *heads, w_out[0], *out,
                far={3 * PLANE + i: pltpu.HBM for i in range(4)},
            )[0]
            for i in range(2)
        ]
        quarters += [swap(quarters[0], 0, 1), swap(after(quarters[1], late[3]), 0, 1)]
        stream, mine, other, kv, tail = call(
            functools.partial(second_kernel, pieces),
            [((rows, width), bf16)] + query_out + keyval_out,
            [((tall, width), bf16), ((tall, width), bf16), weights], 0,
            *quarters, *(late[m] for m in range(pieces)), query_mat,
        )
        kept, given = call(
            functools.partial(attend_kernel, 1), [((tall // 2, part), bf16)] * 2,
            [((tall, part), bf16), ((2 * tall, 2 * part), bf16)],
            attend_flops, mine, swap(other, 1, 0), bias, kv, from_plane_behind(tail),
        )
        mine, other = call(
            pair_kernel, [((tall // 2, part), bf16)] * 2, [], 0, kept, swap(given, 0, 1)
        )
        heads = [mine, swap(other, 0, 2), swap(mine, 1, 0), sooner(swap(other, 1, 2))]
        out = call(
            last_kernel, [((rows, width), bf16)], [((rows, head_width), bf16)],
            2 * rows * head_width * width, *heads, w_out[0], stream,
        )[0]
        return out, bias

    outs = []
    for b in range(batches):
        x, out, bias = inputs[b], None, None
        for tick in range(phases // 2):
            result, bias = two_layers(x, segment_ids[b : b + 1], bias)
            out = result if out is None else jnp.where(phase // 2 == tick, result, out)
            if tick + 1 < phases // 2:
                ahead = [
                    lax.ppermute(result, "phase", [(f, f + d) for f in range(1, phases - d, 2)])
                    for d in (1, 2)
                ]
                x = jnp.where(side == 0, ahead[0], ahead[1])
        outs.append(out)
    return jnp.stack(outs)[None]


def solution(mesh):
    placed = (
        P(None, "ctx", None),
        P(None, "ctx"),
        P("phase", None, None),
        P("phase", "ctx", None),
        P("phase", None, None),
    )
    return jax.shard_map(
        local, mesh=mesh, in_specs=placed, out_specs=P("phase", None, "ctx", None), check_vma=False
    )
```

```python
import functools
import math

import jax
import jax.numpy as jnp
from jax import lax
from jax.experimental import pallas as pl
from jax.experimental.pallas import tpu as pltpu
from jax.sharding import PartitionSpec as P

HEAD = 128
WINDOW = 4
PLANE = 4
FIRST, REST = 11, 5
ORDER = (0, 2, 1, 3)
BOTH = ("phase", "ctx")
VMEM_BYTES = 24 * 1024 * 1024
LONG = 10**11


def swap(block, phase_bit, ctx_bits):
    wide = lax.axis_size("ctx")
    route = [
        (f * wide + d, (f ^ phase_bit) * wide + (d ^ ctx_bits))
        for f in range(lax.axis_size("phase"))
        for d in range(wide)
    ]
    return lax.ppermute(block, BOTH, route)


def from_plane_behind(block):
    wide = lax.axis_size("ctx")
    return lax.ppermute(block, "ctx", [(i, i + PLANE) for i in range(wide - PLANE)])


def rms_rows(values):
    widened = values.astype(jnp.float32)
    scale = lax.rsqrt(jnp.mean(widened * widened, axis=-1, keepdims=True) + 1e-05)
    return (widened * scale).astype(jnp.bfloat16)


def dot(a, b):
    return jnp.dot(a, b, preferred_element_type=jnp.float32)


def call(kernel, outs, scratch, flops, *operands, far={}, vmem=VMEM_BYTES):
    moved = sum(o.size * o.dtype.itemsize for o in operands)
    place = lambda i: far.get(i, pltpu.VMEM)
    return pl.pallas_call(
        kernel,
        out_shape=[jax.ShapeDtypeStruct(s, d) for s, d in outs],
        in_specs=[pl.BlockSpec(memory_space=place(i)) for i in range(len(operands))],
        out_specs=[pl.BlockSpec(memory_space=pltpu.VMEM)] * len(outs),
        scratch_shapes=[pltpu.VMEM(*s) if isinstance(s, tuple) else s for s in scratch],
        cost_estimate=pl.CostEstimate(flops=flops, bytes_accessed=moved, transcendentals=0),
        compiler_params=pltpu.CompilerParams(vmem_limit_bytes=vmem),
    )(*operands)


def extend_kernel(x_ref, id_ref, out_ref):
    rows, width = x_ref.shape
    lanes = out_ref.shape[1] - width
    out_ref[:, :width] = x_ref[...]
    ids = jnp.broadcast_to(id_ref[...].astype(jnp.float32), (rows, rows))
    out_ref[:, width:] = jnp.broadcast_to(
        jnp.transpose(ids)[:, :1], (rows, lanes)
    ).astype(jnp.bfloat16)


def slice_kernel(out_ref, query_ref, sent_first, sent_second, query_mat, sems):
    side = lax.rem(lax.axis_index("phase"), 2)
    own = lax.rem(lax.axis_index("ctx"), PLANE)
    unit, wide = sent_first.shape[0] // FIRST, sent_first.shape[1]
    part = query_mat.shape[1] // 2
    columns = pl.ds(pl.multiple_of(lax.rem(own, 2) * wide, wide), wide)
    copies = []
    for i, (ref, first, count, upper, skip) in enumerate((
        (sent_first, 0, FIRST, own // 2, REST), (sent_second, 0, REST, own // 2, 0),
        (sent_second, REST, REST, 1 - own // 2, 0),
    )):
        at = pl.ds(pl.multiple_of((upper * (FIRST + REST) + skip) * unit, unit), count * unit)
        to = ref.at[pl.ds(first * unit, count * unit)]
        copies.append(pltpu.make_async_copy(out_ref.at[at, columns], to, sems.at[i]))
    for flip in (0, 1):
        at = pl.ds(pl.multiple_of(((side ^ flip) * PLANE + own) * part, part), part)
        to = query_mat.at[:, pl.ds(flip * part, part)]
        copies.append(pltpu.make_async_copy(query_ref.at[:, at], to, sems.at[3 + flip]))
    for copy in copies:
        copy.start()
    for copy in copies:
        copy.wait()


def cut_kernel(w_ref, *out_refs):
    side = lax.rem(lax.axis_index("phase"), 2)
    upper = lax.rem(lax.axis_index("ctx"), PLANE) // 2
    half = w_ref.shape[1] // 2
    pair = out_refs[0].shape[1] // 2
    for ref, (flip_side, flip_upper) in zip(out_refs, ((0, 0), (0, 1), (1, 0), (1, 1))):
        place = ((side ^ flip_side) * 2 + (upper ^ flip_upper)) * pair
        ref[:, :pair] = w_ref[:, pl.ds(pl.multiple_of(place, pair), pair)]
        ref[:, pair:] = w_ref[:, pl.ds(pl.multiple_of(place + half, pair), pair)]


def sort_kernel(kept, across_y, across_x, across_both, near_ref, far_ref):
    side = lax.rem(lax.axis_index("phase"), 2)
    core = lax.rem(lax.axis_index("ctx"), 2)
    rows, part = kept.shape[0], kept.shape[1] // 4
    for layer in range(2):
        for flip, out_ref in enumerate((near_ref, far_ref)):
            head = pl.multiple_of((core ^ flip) * part, part)

            def put(sources):
                for r, ref in enumerate(sources):
                    at = slice(r * rows, (r + 1) * rows)
                    out_ref[layer, at, :part] = ref[:, pl.ds(head, part)]
                    out_ref[layer, at, part:] = ref[:, pl.ds(head + 2 * part, part)]

            pl.when(side == layer)(functools.partial(put, (kept, across_y)))
            pl.when(side != layer)(functools.partial(put, (across_x, across_both)))


def merge_kernel(near_ref, far_ref, early_ref, late_ref):
    rows = near_ref.shape[1]
    for layer, ref in enumerate((early_ref, late_ref)):
        ref[:rows] = near_ref[layer]
        ref[rows:] = far_ref[layer]


def token_kernel(*refs):
    refs[-1][...] = jnp.zeros(refs[-1].shape, refs[-1].dtype)


def copy_kernel(block_ref, out_ref):
    out_ref[...] = block_ref[...]


def fill_weights(ctx, weight_refs, weights):
    rows = weight_refs[0].shape[0] // PLANE
    for m, ref in enumerate(weight_refs):
        for r, o in enumerate(ORDER):
            source = ctx ^ (PLANE * m + o)
            at = pl.ds(pl.multiple_of(source * rows, rows), rows)
            weights[at, :] = ref[r * rows : (r + 1) * rows, :]


def project_query(normed, wq_ref, mine_ref, other_ref):
    queries = dot(normed, wq_ref[...]).astype(jnp.bfloat16)
    part = mine_ref.shape[1]
    mine_ref[...] = queries[:, :part]
    other_ref[...] = queries[:, part:]


def norm_kernel(*refs):
    x_refs, (normed_ref,) = refs[:PLANE], refs[PLANE:]
    rows = x_refs[0].shape[0]
    own = lax.rem(lax.axis_index("ctx"), PLANE)
    for r, o in enumerate(ORDER):
        at = pl.ds(pl.multiple_of((own ^ o) * rows, rows), rows)
        normed_ref[at, :] = rms_rows(x_refs[r][:, : normed_ref.shape[1]])


def group_ids(x_refs, own, group):
    rows, width = x_refs[0].shape[0], x_refs[0].shape[1] - HEAD
    column = jnp.zeros((rows, 1), jnp.float32)
    for r, o in enumerate(ORDER):
        chosen = jnp.where((own ^ o) == group, 1.0, 0.0)
        column = column + chosen * x_refs[r][:, width : width + 1].astype(jnp.float32)
    return jnp.broadcast_to(column, (rows, rows))


def query_kernel(*refs):
    x_refs, (wq_ref, normed_ref, mine_ref, other_ref, ids_ref) = refs[:PLANE], refs[PLANE:]
    own, rows = lax.rem(lax.axis_index("ctx"), PLANE), x_refs[0].shape[0]
    norm_kernel(*x_refs, normed_ref)
    project_query(normed_ref[...], wq_ref, mine_ref, other_ref)
    extra, wide = ids_ref.shape
    line = lax.broadcasted_iota(jnp.int32, (extra, rows), 0)
    block = jnp.zeros((extra, rows), jnp.float32)
    for t in range(WINDOW - 1):
        row = jnp.transpose(group_ids(x_refs, own, PLANE - WINDOW + 1 + t))[:extra]
        block = jnp.where(line == t, row, block)
    ids_ref[:, :rows] = block.astype(jnp.bfloat16)
    ids_ref[:, rows:] = jnp.zeros((extra, wide - rows), jnp.bfloat16)


def keyval_kernel(pieces, *refs):
    weight_refs, (normed_ref, ids_ref, kv_ref, tail_ref, weights) = refs[:pieces], refs[pieces:]
    fill_weights(lax.axis_index("ctx"), weight_refs, weights)
    keyvals = dot(normed_ref[...], weights[...]).astype(jnp.bfloat16)
    kv_ref[...] = keyvals
    past = tail_ref.shape[0] - ids_ref.shape[0]
    tail_ref[:past] = keyvals[keyvals.shape[0] - past :]
    tail_ref[past:] = ids_ref[...]


def out_copies(own, first_column, local_ref, piece_refs, whole, sems):
    first_ref, second_ref, across_ref = piece_refs
    rows, wide = first_ref.shape[0] // FIRST, first_ref.shape[1]
    count_columns = whole.shape[1]
    start = lax.rem(own, 2) * wide + first_column
    columns = pl.ds(pl.multiple_of(start, count_columns), count_columns)
    piece_columns = pl.ds(first_column, count_columns)
    upper, half = own // 2, FIRST + REST
    from_own, from_pieces = [], []
    for i, (ref, first, place, count) in enumerate((
        (first_ref, 0, upper * half + REST, FIRST), (second_ref, 0, upper * half, REST),
        (second_ref, REST, (1 - upper) * half, REST),
        (across_ref, 0, (1 - upper) * half + REST, FIRST),
    )):
        at = pl.ds(pl.multiple_of(place * rows, rows), count * rows)
        source = ref.at[pl.ds(first * rows, count * rows), piece_columns]
        from_own.append(
            pltpu.make_async_copy(local_ref.at[at, columns], whole.at[at], sems.at[i])
        )
        from_pieces.append(pltpu.make_async_copy(source, whole.at[at], sems.at[i]))
    return from_own, from_pieces


def stream_kernel(part_index, *refs):
    x_refs, b_refs = refs[:PLANE], refs[PLANE : 3 * PLANE]
    wo_ref, piece_refs = refs[3 * PLANE], refs[3 * PLANE + 1 : 3 * PLANE + 4]
    half_ref, blended, whole, sems = refs[3 * PLANE + 4 :]
    side = lax.rem(lax.axis_index("phase"), 2)
    own = lax.rem(lax.axis_index("ctx"), PLANE)
    wide = half_ref.shape[1]
    from_own, from_pieces = out_copies(own, part_index * wide, wo_ref, piece_refs, whole, sems)

    @pl.when(side == 0)
    def _():
        for copy in from_own:
            copy.start()

    @pl.when(side == 1)
    def _():
        for copy in from_pieces:
            copy.start()

    rows, part = x_refs[0].shape[0], b_refs[0].shape[1]
    start = (lax.rem(own, 2) * 2 + part_index) * wide
    columns = pl.ds(pl.multiple_of(start, wide), wide)
    for r, o in enumerate(ORDER):
        at = pl.ds(pl.multiple_of((own ^ o) * rows, rows), rows)
        half_ref[at, :] = x_refs[r][:, columns]
    for m, ref in enumerate(b_refs):
        place = (side * PLANE + own) ^ m
        blended[:, pl.ds(pl.multiple_of(place * part, part), part)] = ref[...]
    for copy in from_own:
        copy.wait()
    step = min(512, wide)
    for n in range(0, wide, step):
        total = dot(blended[...], whole[:, n : n + step])
        total = total + half_ref[:, n : n + step].astype(jnp.float32)
        half_ref[:, n : n + step] = total.astype(jnp.bfloat16)


def second_kernel(pieces, *refs):
    quarters, refs = refs[:4], refs[4:]
    weight_refs, refs = refs[:pieces], refs[pieces:]
    wq_ref, own_ref, mine_ref, other_ref, kv_ref, tail_ref, stream, normed, weights = refs
    ctx = lax.axis_index("ctx")
    own, core = lax.rem(ctx, PLANE), lax.rem(ctx, 2)
    rows, wide = own_ref.shape[0], quarters[0].shape[1]
    fill_weights(ctx, weight_refs, weights)
    for i, ref in enumerate(quarters):
        start = ((core ^ (i // 2)) * 2 + i % 2) * wide
        stream[:, pl.ds(pl.multiple_of(start, wide), wide)] = ref[...]
    normed[...] = rms_rows(stream[...])
    own_ref[...] = stream[pl.ds(pl.multiple_of(own * rows, rows), rows), :]
    keyvals = dot(normed[...], weights[...]).astype(jnp.bfloat16)
    kv_ref[...] = keyvals
    tail_ref[...] = keyvals[keyvals.shape[0] - tail_ref.shape[0] :]
    project_query(normed[...], wq_ref, mine_ref, other_ref)


def mask_kernel(*refs):
    x_refs, (past_ref, bias_ref) = refs[:PLANE], refs[PLANE:]
    rows = bias_ref.shape[1]
    ctx = lax.axis_index("ctx")
    own = lax.rem(ctx, PLANE)
    before = WINDOW - 1
    columns = [group_ids(x_refs, own, g) for g in range(PLANE)]
    past = past_ref[before * rows :, :rows].astype(jnp.float32)
    keys = [jnp.broadcast_to(past[t : t + 1], (rows, rows)) for t in range(before)]
    keys += [jnp.transpose(column) for column in columns]
    causal = lax.broadcasted_iota(jnp.int32, (rows, rows), 0) >= lax.broadcasted_iota(
        jnp.int32, (rows, rows), 1
    )
    for g in range(PLANE):
        for t in range(WINDOW):
            allowed = columns[g] == keys[g + t]
            if t == before:
                allowed = allowed & causal
            if g + t < before:
                allowed = allowed & (ctx >= PLANE)
            bias_ref[g, :, t * rows : (t + 1) * rows] = jnp.where(allowed, 0.0, -jnp.inf)


def attend_kernel(layer, mine_ref, got_ref, bias_ref, kv_ref, past_ref, *refs):
    if layer == 0:
        whole, window = refs
    else:
        out_refs, whole, window = refs[:2], refs[2], refs[3]
    rows = bias_ref.shape[1]
    part = mine_ref.shape[1]
    tall, past = kv_ref.shape[0], (WINDOW - 1) * rows
    local_query = lax.rem(lax.axis_index("phase"), 2) == layer
    window[tall - past : tall] = past_ref[:past]
    window[tall:] = kv_ref[...]
    own = lax.rem(lax.axis_index("ctx"), PLANE)
    for g in range(PLANE):
        keys = window[(g + 1) * rows : (g + 1 + WINDOW) * rows]
        for h in range(0, part, HEAD):
            at = (slice(g * rows, (g + 1) * rows), slice(h, h + HEAD))
            query = jnp.where(local_query, mine_ref[at], got_ref[at])
            scores = lax.dot_general(
                query, keys[:, h : h + HEAD], (((1,), (1,)), ((), ())),
                preferred_element_type=jnp.float32,
            )
            scores = scores * (1.0 / math.sqrt(HEAD)) + bias_ref[g]
            weights = jnp.exp(scores - jnp.max(scores, axis=1, keepdims=True))
            total = jnp.sum(weights, axis=1, keepdims=True)
            values = keys[:, part + h : part + h + HEAD]
            result = (dot(weights.astype(jnp.bfloat16), values) / total).astype(jnp.bfloat16)
            whole[g * rows : (g + 1) * rows, h : h + HEAD] = result
    if layer == 0:
        return
    for core, ref in enumerate(out_refs):
        for i in range(2):
            group = 2 * (own // 2 ^ i) + (own % 2 ^ core)
            place = pl.multiple_of(group * rows, rows)
            ref[i * rows : (i + 1) * rows, :] = whole[pl.ds(place, rows), :]


def pair_kernel(kept_ref, got_ref, mine_ref, other_ref):
    rows = kept_ref.shape[0] // 2
    for i, ref in enumerate((mine_ref, other_ref)):
        ref[:rows] = kept_ref[i * rows : (i + 1) * rows]
        ref[rows:] = got_ref[i * rows : (i + 1) * rows]


def last_kernel(*refs):
    b_refs, (wo_ref, own_ref, out_ref, blended) = refs[:PLANE], refs[PLANE:]
    own = lax.rem(lax.axis_index("ctx"), PLANE)
    side = lax.rem(lax.axis_index("phase"), 2)
    rows, part = own_ref.shape[0], b_refs[0].shape[1]

    @pl.when(side == 0)
    def _():
        out_ref[...] = own_ref[...]

    @pl.when(side == 1)
    def _():
        for m in range(2 * PLANE):
            place = pl.multiple_of(((side * PLANE + own) ^ m) * part, part)
            at = slice(m % 2 * rows, (m % 2 + 1) * rows)
            blended[:, pl.ds(place, part)] = b_refs[m // 2][at, :]
        total = own_ref[...].astype(jnp.float32) + dot(blended[...], wo_ref[...])
        out_ref[...] = total.astype(jnp.bfloat16)


def after(value, *others):
    return lax.optimization_barrier((value,) + others)[0]


def token_of(*blocks, cost):
    places = {i: pl.ANY for i in range(len(blocks))}
    return call(token_kernel, [((8, HEAD), jnp.float32)], [], cost, *blocks, far=places)[0]


def sooner(block, cost=4 * 10**8):
    return after(block, token_of(block, cost=cost))


def along_planes(piece, gate=()):
    held = {0: piece, 2: swap(after(piece, *gate), 0, PLANE * 2)}
    for m in range(4, lax.axis_size("ctx") // PLANE):
        held[m] = swap(after(piece, *gate), 0, PLANE * m)
    return held


def local(inputs, segment_ids, w_query, w_keyval, w_out):
    batches, rows, width = inputs.shape
    phases = lax.axis_size("phase")
    phase = lax.axis_index("phase")
    side = phase % 2
    own = lax.axis_index("ctx") % PLANE
    bf16 = jnp.bfloat16

    head_width = w_query.shape[2]
    part = head_width // (2 * PLANE)
    depth = w_keyval.shape[1]
    tall, past = PLANE * rows, (WINDOW - 1) * rows

    unit, half = head_width // (2 * (FIRST + REST)), width // 2
    sent_first, sent_second, query_mat = call(
        slice_kernel,
        [((FIRST * unit, half), bf16), ((2 * REST * unit, half), bf16), ((width, 2 * part), bf16)],
        [pltpu.SemaphoreType.DMA((5,))], LONG, w_out[0], w_query[0], far={0: pltpu.HBM, 1: pltpu.HBM}, vmem=60 * 1024 * 1024,
    )

    kept, for_y, for_x, for_both = call(
        cut_kernel, [((depth, 4 * part), bf16)] * 4, [], 0, w_keyval[0]
    )
    across_both, across_x, across_y = swap(for_both, 1, 2), swap(for_x, 1, 0), swap(for_y, 0, 2)
    kept, sent_first, sent_second, query_mat = lax.optimization_barrier(
        (kept, sent_first, sent_second, query_mat)
    )
    near, far = call(
        sort_kernel, [((2, 2 * depth, 2 * part), bf16)] * 2, [], 0,
        kept, across_y, across_x, across_both,
    )
    piece = (4 * depth, 2 * part)
    early, late_start = call(
        merge_kernel, [(piece, bf16)] * 2, [], 0, near, swap(far, 0, 1)
    )
    out_first = swap(after(sent_first, across_y), 1, 0)
    shared = {}
    sent_on = call(copy_kernel, [((FIRST * unit, half), bf16)], [], 6 * 10**9, out_first)[0]
    out_across = swap(sent_on, 0, 2)
    early = along_planes(early)
    early[1] = swap(early[0], 0, PLANE)
    ready = token_of(token_of(early[2], cost=4 * 10**8), early[1], cost=35 * 10**8)
    early[3] = swap(after(early[2], ready), 0, PLANE)
    pieces = len(early)

    keyval_out = [((tall, 2 * part), bf16), ((past, 2 * part), bf16)]
    first_out = [((tall, 2 * part), bf16), ((past + 16, 2 * part), bf16)]
    query_out = [((tall, part), bf16)] * 2
    weights = ((width, 2 * part), bf16)
    dot_flops = 2 * tall * width * 2 * part
    attend_flops = 4 * tall * WINDOW * rows * part

    def two_layers(x, ids, bias):
        x = call(extend_kernel, [((rows, width + HEAD), bf16)], [], 0, x, ids)[0]
        across = swap(after(x, early[0]), 0, 2)
        xs = [x, across] + [swap(after(b, ready), 0, 1) for b in (x, across)]
        normed, mine, other, ids = call(
            query_kernel, [((tall, width), bf16)] + query_out + [((16, 2 * part), bf16)], [], 0,
            *xs, query_mat,
        )
        if not shared:
            shared["out"] = swap(after(sent_second, mine), 1, 0)
        kv, tail = call(
            functools.partial(keyval_kernel, pieces), first_out, [weights], LONG,
            *(early[m] for m in range(pieces)), normed, ids,
        )
        query = swap(other, 1, 0)
        late = along_planes(late_start, (kv,))
        late[1] = swap(after(late_start, kv), 0, PLANE)
        past_kv = from_plane_behind(tail)
        if bias is None:
            shape = ((PLANE, rows, WINDOW * rows), jnp.float32)
            bias = call(mask_kernel, [shape], [], 6 * 10**8, *xs, after(past_kv, query))[0]
        bias, first, across_out = lax.optimization_barrier((bias, out_first, out_across))
        blended = call(
            functools.partial(attend_kernel, 0), [((tall, part), bf16)],
            [((2 * tall, 2 * part), bf16)], 0, mine, query, bias, kv, past_kv,
        )[0]
        y_block, second = lax.optimization_barrier((blended, shared["out"]))
        out = [first, second, across_out]
        near = [blended, swap(y_block, 0, 2), swap(blended, 1, 0), sooner(swap(blended, 1, 2))]
        heads = [b for n in near for b in (n, swap(n, 0, 1))]
        late[3] = swap(after(late[2], late[1], near[3]), 0, PLANE)
        quarters = [
            call(
                functools.partial(stream_kernel, i), [((tall, width // 4), bf16)],
                [((tall, head_width), bf16), ((head_width, width // 4), bf16),
                 pltpu.SemaphoreType.DMA((4,))],
                0, *xs, *heads, w_out[0], *out,
                far={3 * PLANE + i: pltpu.HBM for i in range(4)},
            )[0]
            for i in range(2)
        ]
        quarters += [swap(quarters[0], 0, 1), swap(after(quarters[1], late[3]), 0, 1)]
        stream, mine, other, kv, tail = call(
            functools.partial(second_kernel, pieces),
            [((rows, width), bf16)] + query_out + keyval_out,
            [((tall, width), bf16), ((tall, width), bf16), weights], 0,
            *quarters, *(late[m] for m in range(pieces)), query_mat,
        )
        kept, given = call(
            functools.partial(attend_kernel, 1), [((tall // 2, part), bf16)] * 2,
            [((tall, part), bf16), ((2 * tall, 2 * part), bf16)],
            attend_flops, mine, swap(other, 1, 0), bias, kv, from_plane_behind(tail),
        )
        mine, other = call(
            pair_kernel, [((tall // 2, part), bf16)] * 2, [], 0, kept, swap(given, 0, 1)
        )
        heads = [mine, swap(other, 0, 2), swap(mine, 1, 0), sooner(swap(other, 1, 2))]
        out = call(
            last_kernel, [((rows, width), bf16)], [((rows, head_width), bf16)],
            2 * rows * head_width * width, *heads, w_out[0], stream,
        )[0]
        return out, bias

    outs = []
    for b in range(batches):
        x, out, bias = inputs[b], None, None
        for tick in range(phases // 2):
            result, bias = two_layers(x, segment_ids[b : b + 1], bias)
            out = result if out is None else jnp.where(phase // 2 == tick, result, out)
            if tick + 1 < phases // 2:
                ahead = [
                    lax.ppermute(result, "phase", [(f, f + d) for f in range(1, phases - d, 2)])
                    for d in (1, 2)
                ]
                x = jnp.where(side == 0, ahead[0], ahead[1])
        outs.append(out)
    return jnp.stack(outs)[None]


def solution(mesh):
    placed = (
        P(None, "ctx", None),
        P(None, "ctx"),
        P("phase", None, None),
        P("phase", "ctx", None),
        P("phase", None, None),
    )
    return jax.shard_map(
        local, mesh=mesh, in_specs=placed, out_specs=P("phase", None, "ctx", None), check_vma=False
    )
```
